32 devices in a mesh: row: 8 (over y, x, core), col: 4 (over z).
Axes of the slice: x: 2, y: 2, z: 4, core: 2. Of those that a mesh axis runs over, the one named last changes fastest.
Arguments:
- support: bfloat16 [8192, 4096], P(('row', 'col')), may hold values from -6 to 6
- targets: bfloat16 [256, 4096], P('col'), may hold values from -6 to 6
- panels: float32 [2, 128, 8192], P(None, None, ('row', 'col')), may hold values from -0.21875 to 0.21875
- diag_inverses: float32 [2, 128, 128], replicated, may hold values from -1 to 1.5, as said below
Outputs:
- solved: float32 [256, 8192], P('col', 'row')
The draws below stay inside these ranges and needn't reach their ends.
Inputs may be any that keep to these rules, and one draw needn't show every extreme that they name: Each diag_inverses[k] is lower triangular.
All inputs are finite; a program needn't handle non-finite values.
Results may differ from the reference program's by a relative error of at most 0.0003.
Values may be sent and summed in bfloat16 or wider, within the bound.
No kernel may reach another device: no remote copies, remote signals or barrier semaphores. Data moves between devices by JAX's collectives and lax.ppermute only.
A program may use at most 64 MiB of HBM per device.

```python
import math
import jax
import jax.numpy as jnp
from jax import lax

FEAT = 4096
PANEL = 128
ROWS_DEV = 256
SUPPORT = 8192
TARGETS = 256
N_ROW = 8
N_COL = 4


def feature_draw(key, count):
    values = jax.random.truncated_normal(key, -6.0, 6.0, (count, FEAT), jnp.float32)
    return values.astype(jnp.bfloat16)


def draw_support(key, part):
    return feature_draw(jax.random.fold_in(key, 3), SUPPORT)


def draw_targets(key, part):
    return feature_draw(jax.random.fold_in(key, 7), TARGETS)


def draw_diag_inverses(key, part):
    first_key, second_key = jax.random.split(jax.random.fold_in(key, 11))
    lower = jnp.tril(jnp.ones((PANEL, PANEL), jnp.float32), -1)
    identity = jnp.eye(PANEL, dtype=jnp.float32)
    spread = 0.5 * jax.random.truncated_normal(first_key, -4.0, 4.0, (2, PANEL, PANEL), jnp.float32)
    diagonal = jax.random.uniform(second_key, (2, PANEL, PANEL), jnp.float32, 0.6, 1.4)
    return lower * spread * (1.0 / math.sqrt(PANEL)) + identity * diagonal


def block_scale(stream_key, dims, cuts, smallest, largest):
    loudness, own = 1.0, jax.random.fold_in(stream_key, 6)
    for position, blocks in cuts:
        steps = jnp.exp(jax.random.uniform(jax.random.fold_in(own, position), (blocks,), jnp.float32, smallest / len(cuts), largest / len(cuts)))
        loudness = loudness * jnp.repeat(steps, dims[position] // blocks).reshape([-1 if axis == position else 1 for axis in range(len(dims))])
    return loudness


def noise(rng, dims, deviation, bound, shards=(), kind=jnp.bfloat16):
    level = block_scale(rng, dims, shards, -0.22, 0.18) if shards else 1.0
    array = jax.random.normal(rng, dims, jnp.float32) * deviation * level
    return jnp.minimum(jnp.maximum(array, -bound), bound).astype(kind)


def setup_inputs(seed: int = 0) -> dict:
    splits = jax.random.split(jax.random.key(seed), 5)
    support = draw_support(jax.random.fold_in(splits[4], 71), 0)
    targets = draw_targets(jax.random.fold_in(splits[4], 71), 0)
    panels = noise(splits[2], (2, PANEL, SUPPORT), (6 * PANEL) ** -0.5, 0.21875, ((2, 32),), jnp.float32)
    diag_inverses = draw_diag_inverses(jax.random.fold_in(splits[4], 71), 0)
    return {"support": support, "targets": targets, "panels": panels, "diag_inverses": diag_inverses}


def reference(support, targets, panels, diag_inverses):
    feature_width = support.shape[1]
    kernel_scale = 0.5 / math.sqrt(feature_width)
    grid_span = ROWS_DEV * N_COL
    pivot_width = diag_inverses.shape[1]

    def form_block(support_rows):
        products = jnp.dot(targets, support_rows.T, preferred_element_type=jnp.float32)
        return jnp.exp(kernel_scale * products)
    blocks = support.reshape(N_ROW, grid_span, feature_width)
    kernel = lax.map(form_block, blocks)
    kernel = jnp.transpose(kernel, (1, 0, 2)).reshape(targets.shape[0], support.shape[0])
    for panel_num in range(2):
        lower = panel_num * grid_span
        kept_heads = [kernel[:, earlier * grid_span:earlier * grid_span + pivot_width] for earlier in range(panel_num)]
        pivot_cols = kernel[:, lower:lower + pivot_width]
        solved_head = jnp.dot(pivot_cols, diag_inverses[panel_num].T, precision=lax.Precision.HIGHEST, preferred_element_type=jnp.float32)
        kernel = kernel - jnp.dot(solved_head, panels[panel_num], precision=lax.Precision.HIGHEST, preferred_element_type=jnp.float32)
        kernel = kernel.at[:, lower:lower + pivot_width].set(solved_head)
        for earlier in range(panel_num):
            kernel = kernel.at[:, earlier * grid_span:earlier * grid_span + pivot_width].set(kept_heads[earlier])
    return kernel
```

```python
import functools
import math

import jax
import jax.numpy as jnp
from jax import lax
from jax.experimental import pallas as pl
from jax.experimental.pallas import tpu as pltpu
from jax.sharding import PartitionSpec as P

VMEM = pl.BlockSpec(memory_space=pltpu.VMEM)
HBM = pl.BlockSpec(memory_space=pltpu.HBM)
PARAMS = pltpu.CompilerParams(vmem_limit_bytes=60 * 2**20)
LONG = pl.CostEstimate(flops=50_000_000_000, bytes_accessed=0, transcendentals=0)
SHORT = pl.CostEstimate(flops=1_000_000, bytes_accessed=0, transcendentals=0)
PANEL_UNIT = 2.0**17
NT = (((1,), (1,)), ((), ()))
TN = (((0,), (0,)), ((), ()))
NN = (((1,), (0,)), ((), ()))


def dot(a, b, dims):
    return lax.dot_general(a, b, dims, preferred_element_type=jnp.float32)


def halves(a):
    high = a.astype(jnp.bfloat16)
    return high, (a - high.astype(jnp.float32)).astype(jnp.bfloat16)


def dot32(a, b, dims):
    (a_high, a_low), (b_high, b_low) = halves(a), halves(b)
    return dot(a_high, b_high, dims) + (dot(a_low, b_high, dims) + dot(a_high, b_low, dims))


def slice_of(row, n_row):
    return (row % 2) * (n_row // 2) + row // 2


def start_all(pairs, sems):
    copies = [pltpu.make_async_copy(source, target, sems.at[i]) for i, (source, target) in enumerate(pairs)]
    for copy in copies:
        copy.start()
    return copies


def wait_all(copies):
    for copy in copies:
        copy.wait()


def corner_kernel(corner_ref, out_ref):
    out_ref[...] = corner_ref[0]


def tile_kernel(scale, n_row, n_col, *refs):
    own_hbm, support_hbm, sibling_hbm, corner_ref, inverse_ref = refs[:5]
    near, far, refs = refs[5:7], refs[7:7 + n_row], refs[7 + n_row:]
    outs, (targets_ref, support_ref, sems) = refs[:n_col], refs[n_col:]
    (rows, features), (_, width) = own_hbm.shape, far[0].shape
    span, pivot = support_hbm.shape[0], corner_ref.shape[1]
    half = features // 2
    row, col = lax.axis_index("row"), lax.axis_index("col")
    odd = row % 2
    steps = []
    for core in range(2):
        cols = pl.ds(pl.multiple_of((odd ^ core) * half, half), half)
        loads = [
            (own_hbm.at[:, cols], targets_ref.at[pl.ds(0, rows), cols]),
            (support_hbm.at[:, cols], support_ref.at[pl.ds(0, span), cols]),
            (sibling_hbm.at[pl.ds(0, pivot), cols], support_ref.at[pl.ds(span, pivot), cols]),
            (near[core], targets_ref.at[pl.ds(rows, rows), cols]),
        ]
        for step in range(core, n_row, 2):
            inner = pl.ds(pl.multiple_of(slice_of(row ^ step, n_row) * width, width), width)
            loads.append((far[step], targets_ref.at[pl.ds(2 * rows, far[step].shape[0]), inner]))
        steps.append((cols, start_all(loads, sems.at[core])))
    total = 0.0
    for cols, copies in steps:
        wait_all(copies)
        total = total + dot(targets_ref[:, cols], support_ref[:, cols], NT)
    kernel = jnp.exp(scale * total)
    other = jnp.where(odd == 1, kernel[:, span:], 0.0)
    head = kernel[:, :pivot] - dot32(dot32(other, inverse_ref[0], NT), corner_ref[...], NN)
    head = dot32(head, inverse_ref[odd], NT)
    for plane in range(n_col):
        part = slice(plane * rows, (plane + 1) * rows)
        outs[plane][:, :span] = kernel[part, :span]
        outs[plane][:, span:] = head[part]


def solve_kernel(n_col, pivot, *refs):
    tiles, (own_ref, panels_ref, mine_ref, other_ref, out_ref) = refs[:n_col], refs[n_col:]
    span = own_ref.shape[2]
    row, col = lax.axis_index("row"), lax.axis_index("col")
    even = row % 2 == 0
    mine, other = mine_ref[...], other_ref[...]
    first = jnp.where(even, mine, other)
    second = jnp.where(even, other, mine)
    for step in range(n_col):
        plane = col ^ step
        block = own_ref if step == 0 else panels_ref.at[plane]
        value = tiles[step][:, :span] - dot32(first, block[0], NN) - dot32(second, block[1], NN)
        out_ref[:, pl.ds(pl.multiple_of(plane * span, span), span)] = value

    @pl.when(row == 0)
    def _():
        out_ref[:, :pivot] = first

    @pl.when(row == 1)
    def _():
        out_ref[:, :pivot] = second


def exchange(value, axis, size, mask):
    return lax.ppermute(value, axis, [(i, i ^ mask) for i in range(size)])


def together(*values):
    return lax.optimization_barrier(values)


def shards(support, targets, panels, diag_inverses, *, n_row, n_col):
    rows, features = targets.shape
    span = support.shape[0]
    pivot = diag_inverses.shape[1]
    scale = 0.5 / math.sqrt(features)
    row, col = lax.axis_index("row"), lax.axis_index("col")
    width = features // n_row

    half = lax.dynamic_slice(targets, (0, (row % 2) * (features // 2)), (rows, features // 2))
    mine = lax.dynamic_slice(targets, (0, slice_of(row, n_row) * width), (rows, width))
    sibling = exchange(support, "row", n_row, 1)
    near = exchange(half, "col", n_col, 1)
    far = jnp.concatenate([exchange(mine, "col", n_col, j) for j in range(2, n_col)], axis=0)
    small = (jnp.broadcast_to(panels, (n_col, *panels.shape)) * PANEL_UNIT).astype(jnp.float16)
    blocks = lax.all_to_all(small, "col", 0, 0)
    corner = pl.pallas_call(
        corner_kernel,
        grid=(1,),
        out_shape=jax.ShapeDtypeStruct((pivot, pivot), jnp.float32),
        in_specs=[pl.BlockSpec((1, pivot, pivot), lambda i: (0, 0, 0))],
        out_specs=VMEM,
        compiler_params=PARAMS,
        cost_estimate=LONG,
        name="corner_kernel",
    )(panels)
    far, corner = together(far, corner)
    near = [near, exchange(near, "row", n_row, 1)]
    far = [far] + [exchange(far, "row", n_row, i) for i in range(2, n_row, 2)]
    far = [p for own in far for p in (own, exchange(own, "row", n_row, 1))]
    near[0], blocks = together(near[0], blocks)

    made = pl.pallas_call(
        functools.partial(tile_kernel, scale, n_row, n_col),
        out_shape=[jax.ShapeDtypeStruct((rows, span + pivot), jnp.float32)] * n_col,
        in_specs=[HBM] * 3 + [VMEM] * 2 + [HBM] * (n_row + 2),
        out_specs=[VMEM] * n_col,
        scratch_shapes=[
            pltpu.VMEM((n_col * rows, features), jnp.bfloat16),
            pltpu.VMEM((span + pivot, features), jnp.bfloat16),
            pltpu.SemaphoreType.DMA((2, n_row + 4)),
        ],
        compiler_params=PARAMS,
        cost_estimate=SHORT,
        name="tile_kernel",
    )(targets, support, sibling, corner, diag_inverses, *near, *far)

    tiles = [made[0]] + [exchange(made[j], "col", n_col, j) for j in range(1, n_col)]
    head = tiles[0][:, span:]
    for j in range(1, n_col):
        head = jnp.where(col == j, tiles[j][:, span:], head)
    spread = jnp.where(row < 2, head, 0.0)
    for i in range(2, n_row, 2):
        pairs = [(k * n_col + c, (i + k) * n_col + c) for k in range(2) for c in range(n_col)]
        spread = spread + lax.ppermute(head, ("row", "col"), pairs)
    swapped = exchange(spread, "row", n_row, 1)
    blocks = blocks.astype(jnp.float32) * (1 / PANEL_UNIT)

    return pl.pallas_call(
        functools.partial(solve_kernel, n_col, pivot),
        out_shape=jax.ShapeDtypeStruct((rows, span * n_col), jnp.float32),
        in_specs=[VMEM] * (n_col + 4),
        out_specs=VMEM,
        compiler_params=PARAMS,
        name="solve_kernel",
    )(*tiles, panels, blocks, spread, swapped)


def solution(mesh):
    in_specs = (P(("row", "col"), None), P("col", None), P(None, None, ("row", "col")), P())
    body = functools.partial(shards, n_row=mesh.shape["row"], n_col=mesh.shape["col"])
    return jax.shard_map(body, mesh=mesh, in_specs=in_specs, out_specs=P("col", "row"), check_vma=False)
```

```python
import functools
import math

import jax
import jax.numpy as jnp
from jax import lax
from jax.experimental import pallas as pl
from jax.experimental.pallas import tpu as pltpu
from jax.sharding import PartitionSpec as P

VMEM = pl.BlockSpec(memory_space=pltpu.VMEM)
HBM = pl.BlockSpec(memory_space=pltpu.HBM)
TILE_PARAMS = pltpu.CompilerParams(vmem_limit_bytes=32 * 2**20)
SOLVE_PARAMS = pltpu.CompilerParams(vmem_limit_bytes=32 * 2**20)
LONG = pl.CostEstimate(flops=50_000_000_000, bytes_accessed=0, transcendentals=0)
SHORT = pl.CostEstimate(flops=1_000_000, bytes_accessed=0, transcendentals=0)
PANEL_UNIT = 2.0**17
NT = (((1,), (1,)), ((), ()))
TN = (((0,), (0,)), ((), ()))
NN = (((1,), (0,)), ((), ()))


def dot(a, b, dims):
    return lax.dot_general(a, b, dims, preferred_element_type=jnp.float32)


def halves(a):
    high = a.astype(jnp.bfloat16)
    return high, (a - high.astype(jnp.float32)).astype(jnp.bfloat16)


def dot32(a, b, dims):
    (a_high, a_low), (b_high, b_low) = halves(a), halves(b)
    return dot(a_high, b_high, dims) + (dot(a_low, b_high, dims) + dot(a_high, b_low, dims))


def slice_of(row, n_row):
    return (row % 2) * (n_row // 2) + row // 2


def start_all(pairs, sems):
    copies = [pltpu.make_async_copy(source, target, sems.at[i]) for i, (source, target) in enumerate(pairs)]
    for copy in copies:
        copy.start()
    return copies


def wait_all(copies):
    for copy in copies:
        copy.wait()


def mark_kernel(value_ref, token_ref, out_ref):
    del token_ref
    out_ref[...] = value_ref[0, :8, :128]


def tile_kernel(scale, n_row, n_col, own_hbm, support_hbm, _, *refs):
    near, far, refs = refs[:2], refs[2:2 + n_row], refs[2 + n_row:]
    outs, (targets_ref, support_ref, sems) = refs[:n_col], refs[n_col:]
    (rows, features), (_, width) = own_hbm.shape, far[0].shape
    half = features // 2
    row = lax.axis_index("row")
    odd = row % 2
    steps = []
    for core in range(2):
        cols = pl.ds(pl.multiple_of((odd ^ core) * half, half), half)
        loads = [
            (own_hbm.at[:, cols], targets_ref.at[pl.ds(0, rows), cols]),
            (support_hbm.at[:, cols], support_ref.at[:, cols]),
            (near[core], targets_ref.at[pl.ds(rows, rows), cols]),
        ]
        for step in range(core, n_row, 2):
            inner = pl.ds(pl.multiple_of(slice_of(row ^ step, n_row) * width, width), width)
            loads.append((far[step], targets_ref.at[pl.ds(2 * rows, far[step].shape[0]), inner]))
        steps.append((cols, start_all(loads, sems.at[core])))
    total = 0.0
    for cols, copies in steps:
        wait_all(copies)
        total = total + dot(targets_ref[:, cols], support_ref[:, cols], NT)
    for plane in range(n_col):
        outs[plane][...] = jnp.exp(scale * total[plane * rows:(plane + 1) * rows])


def head_kernel(mine_ref, other_ref, corner_ref, inverse_ref, out_ref):
    odd = lax.axis_index("row") % 2
    other = jnp.where(odd == 1, other_ref[...], 0.0)
    head = mine_ref[...] - dot32(dot32(other, inverse_ref[0], NT), corner_ref[...], NN)
    out_ref[...] = dot32(head, inverse_ref[odd], NT)


def solve_kernel(n_col, pivot, *refs):
    tiles, (own_ref, panels_ref, mine_ref, other_ref, out_ref) = refs[:n_col], refs[n_col:]
    span = own_ref.shape[2]
    row, col = lax.axis_index("row"), lax.axis_index("col")
    even = row % 2 == 0
    mine, other = mine_ref[...], other_ref[...]
    first = jnp.where(even, mine, other)
    second = jnp.where(even, other, mine)
    for step in range(n_col):
        plane = col ^ step
        block = own_ref if step == 0 else panels_ref.at[plane]
        value = tiles[step][...] - dot32(first, block[0], NN) - dot32(second, block[1], NN)
        out_ref[:, pl.ds(pl.multiple_of(plane * span, span), span)] = value

    @pl.when(row == 0)
    def _():
        out_ref[:, :pivot] = first

    @pl.when(row == 1)
    def _():
        out_ref[:, :pivot] = second


def exchange(value, axis, size, mask):
    return lax.ppermute(value, axis, [(i, i ^ mask) for i in range(size)])


def together(*values):
    return lax.optimization_barrier(values)


def shards(support, targets, panels, diag_inverses, *, n_row, n_col):
    rows, features = targets.shape
    span = support.shape[0]
    pivot = diag_inverses.shape[1]
    scale = 0.5 / math.sqrt(features)
    row, col = lax.axis_index("row"), lax.axis_index("col")
    width = features // n_row

    half = lax.dynamic_slice(targets, (0, (row % 2) * (features // 2)), (rows, features // 2))
    mine = lax.dynamic_slice(targets, (0, slice_of(row, n_row) * width), (rows, width))
    near = exchange(half, "col", n_col, 1)
    far = jnp.concatenate([exchange(mine, "col", n_col, j) for j in range(2, n_col)], axis=0)
    small = jnp.concatenate([panels * PANEL_UNIT] * n_col, axis=0).astype(jnp.float16)
    small = small.reshape(n_col, *panels.shape)
    far, small, marked = together(far, small, diag_inverses)
    token = exchange(far[:16, :128], "row", n_row, 1)
    small, token = together(small, token)
    blocks = lax.all_to_all(small, "col", 0, 0)
    mark = pl.pallas_call(
        mark_kernel,
        grid=(1,),
        out_shape=jax.ShapeDtypeStruct((8, 128), jnp.float32),
        in_specs=[pl.BlockSpec((1, 8, 128), lambda i: (0, 0, 0)), VMEM],
        out_specs=VMEM,
        compiler_params=SOLVE_PARAMS,
        cost_estimate=LONG,
        name="mark_kernel",
    )(marked, token)
    near = [near, exchange(near, "row", n_row, 1)]
    far = [far] + [exchange(far, "row", n_row, i) for i in range(2, n_row, 2)]
    far[1], mark = together(far[1], mark)
    far = [p for own in far for p in (own, exchange(own, "row", n_row, 1))]

    made = pl.pallas_call(
        functools.partial(tile_kernel, scale, n_row, n_col),
        out_shape=[jax.ShapeDtypeStruct((rows, span), jnp.float32)] * n_col,
        in_specs=[HBM] * (n_row + 5),
        out_specs=[VMEM] * n_col,
        scratch_shapes=[
            pltpu.VMEM((n_col * rows, features), jnp.bfloat16),
            pltpu.VMEM((span, features), jnp.bfloat16),
            pltpu.SemaphoreType.DMA((2, n_row + 4)),
        ],
        compiler_params=TILE_PARAMS,
        cost_estimate=SHORT,
        name="tile_kernel",
    )(targets, support, mark, *near, *far)

    tiles = [made[0]] + [exchange(made[j], "col", n_col, j) for j in range(1, n_col)]
    tiles, blocks = together(tiles, blocks)
    corner = blocks[0, 0, :, :pivot].astype(jnp.float32) * (1 / PANEL_UNIT)
    head = tiles[0][:, :pivot]
    for j in range(1, n_col):
        head = jnp.where(col == j, tiles[j][:, :pivot], head)
    head = pl.pallas_call(
        head_kernel,
        out_shape=jax.ShapeDtypeStruct((rows, pivot), jnp.float32),
        in_specs=[VMEM] * 4,
        out_specs=VMEM,
        compiler_params=SOLVE_PARAMS,
        cost_estimate=SHORT,
        name="head_kernel",
    )(head, exchange(head, "row", n_row, 1), corner, diag_inverses)
    spread = head
    for i in range(2, n_row, 2):
        spread = jnp.where(row // 2 == i // 2, exchange(head, "row", n_row, i), spread)
    swapped = exchange(spread, "row", n_row, 1)
    blocks = blocks.astype(jnp.float32) * (1 / PANEL_UNIT)

    return pl.pallas_call(
        functools.partial(solve_kernel, n_col, pivot),
        out_shape=jax.ShapeDtypeStruct((rows, span * n_col), jnp.float32),
        in_specs=[VMEM] * (n_col + 4),
        out_specs=VMEM,
        compiler_params=SOLVE_PARAMS,
        name="solve_kernel",
    )(*tiles, panels, blocks, spread, swapped)


def solution(mesh):
    in_specs = (P(("row", "col"), None), P("col", None), P(None, None, ("row", "col")), P())
    body = functools.partial(shards, n_row=mesh.shape["row"], n_col=mesh.shape["col"])
    return jax.shard_map(body, mesh=mesh, in_specs=in_specs, out_specs=P("col", "row"), check_vma=False)
```

```python
import functools
import math

import jax
import jax.numpy as jnp
from jax import lax
from jax.experimental import pallas as pl
from jax.experimental.pallas import tpu as pltpu
from jax.sharding import PartitionSpec as P

VMEM = pl.BlockSpec(memory_space=pltpu.VMEM)
HBM = pl.BlockSpec(memory_space=pltpu.HBM)
TILE_PARAMS = pltpu.CompilerParams(vmem_limit_bytes=32 * 2**20)
SOLVE_PARAMS = pltpu.CompilerParams(vmem_limit_bytes=32 * 2**20)
LONG = pl.CostEstimate(flops=50_000_000_000, bytes_accessed=0, transcendentals=0)
SHORT = pl.CostEstimate(flops=1_000_000, bytes_accessed=0, transcendentals=0)
PANEL_UNIT = 2.0**17
NT = (((1,), (1,)), ((), ()))
TN = (((0,), (0,)), ((), ()))
NN = (((1,), (0,)), ((), ()))


def dot(a, b, dims):
    return lax.dot_general(a, b, dims, preferred_element_type=jnp.float32)


def halves(a):
    high = a.astype(jnp.bfloat16)
    return high, (a - high.astype(jnp.float32)).astype(jnp.bfloat16)


def dot32(a, b, dims):
    (a_high, a_low), (b_high, b_low) = halves(a), halves(b)
    return dot(a_high, b_high, dims) + (dot(a_low, b_high, dims) + dot(a_high, b_low, dims))


def slice_of(row, n_row):
    return (row % 2) * (n_row // 2) + row // 2


def start_all(pairs, sems):
    copies = [pltpu.make_async_copy(source, target, sems.at[i]) for i, (source, target) in enumerate(pairs)]
    for copy in copies:
        copy.start()
    return copies


def wait_all(copies):
    for copy in copies:
        copy.wait()


def mark_kernel(value_ref, out_ref):
    out_ref[...] = value_ref[0, :8, :128]


def tile_kernel(scale, n_row, n_col, own_hbm, support_hbm, _, *refs):
    near, far, refs = refs[:2], refs[2:2 + n_row], refs[2 + n_row:]
    outs, (targets_ref, support_ref, sems) = refs[:n_col], refs[n_col:]
    (rows, features), (_, width) = own_hbm.shape, far[0].shape
    half = features // 2
    row = lax.axis_index("row")
    odd = row % 2
    steps = []
    for core in range(2):
        cols = pl.ds(pl.multiple_of((odd ^ core) * half, half), half)
        loads = [
            (own_hbm.at[:, cols], targets_ref.at[pl.ds(0, rows), cols]),
            (support_hbm.at[:, cols], support_ref.at[:, cols]),
            (near[core], targets_ref.at[pl.ds(rows, rows), cols]),
        ]
        for step in range(core, n_row, 2):
            inner = pl.ds(pl.multiple_of(slice_of(row ^ step, n_row) * width, width), width)
            loads.append((far[step], targets_ref.at[pl.ds(2 * rows, far[step].shape[0]), inner]))
        steps.append((cols, start_all(loads, sems.at[core])))
    total = 0.0
    for cols, copies in steps:
        wait_all(copies)
        total = total + dot(targets_ref[:, cols], support_ref[:, cols], NT)
    for plane in range(n_col):
        outs[plane][...] = jnp.exp(scale * total[plane * rows:(plane + 1) * rows])


def head_kernel(mine_ref, other_ref, corner_ref, inverse_ref, out_ref):
    odd = lax.axis_index("row") % 2
    other = jnp.where(odd == 1, other_ref[...], 0.0)
    head = mine_ref[...] - dot32(dot32(other, inverse_ref[0], NT), corner_ref[...], NN)
    out_ref[...] = dot32(head, inverse_ref[odd], NT)


def solve_kernel(n_col, pivot, *refs):
    tiles, (own_ref, panels_ref, mine_ref, other_ref, out_ref) = refs[:n_col], refs[n_col:]
    span = own_ref.shape[2]
    row, col = lax.axis_index("row"), lax.axis_index("col")
    even = row % 2 == 0
    mine, other = mine_ref[...], other_ref[...]
    first = jnp.where(even, mine, other)
    second = jnp.where(even, other, mine)
    for step in range(n_col):
        plane = col ^ step
        block = own_ref if step == 0 else panels_ref.at[plane]
        value = tiles[step][...] - dot32(first, block[0], NN) - dot32(second, block[1], NN)
        out_ref[:, pl.ds(pl.multiple_of(plane * span, span), span)] = value

    @pl.when(row == 0)
    def _():
        out_ref[:, :pivot] = first

    @pl.when(row == 1)
    def _():
        out_ref[:, :pivot] = second


def exchange(value, axis, size, mask):
    return lax.ppermute(value, axis, [(i, i ^ mask) for i in range(size)])


def together(*values):
    return lax.optimization_barrier(values)


def shards(support, targets, panels, diag_inverses, *, n_row, n_col):
    rows, features = targets.shape
    span = support.shape[0]
    pivot = diag_inverses.shape[1]
    scale = 0.5 / math.sqrt(features)
    row, col = lax.axis_index("row"), lax.axis_index("col")
    width = features // n_row

    half = lax.dynamic_slice(targets, (0, (row % 2) * (features // 2)), (rows, features // 2))
    mine = lax.dynamic_slice(targets, (0, slice_of(row, n_row) * width), (rows, width))
    near = exchange(half, "col", n_col, 1)
    far = jnp.concatenate([exchange(mine, "col", n_col, j) for j in range(2, n_col)], axis=0)
    small = jnp.concatenate([panels * PANEL_UNIT] * n_col, axis=0).astype(jnp.float16)
    small = small.reshape(n_col, *panels.shape)
    blocks = lax.all_to_all(small, "col", 0, 0)
    mark = pl.pallas_call(
        mark_kernel,
        grid=(1,),
        out_shape=jax.ShapeDtypeStruct((8, 128), jnp.float32),
        in_specs=[pl.BlockSpec((1, 8, 128), lambda i: (0, 0, 0))],
        out_specs=VMEM,
        compiler_params=SOLVE_PARAMS,
        cost_estimate=LONG,
        name="mark_kernel",
    )(diag_inverses)
    far, mark = together(far, mark)
    near = [near, exchange(near, "row", n_row, 1)]
    far = [far] + [exchange(far, "row", n_row, i) for i in range(2, n_row, 2)]
    far = [p for own in far for p in (own, exchange(own, "row", n_row, 1))]

    made = pl.pallas_call(
        functools.partial(tile_kernel, scale, n_row, n_col),
        out_shape=[jax.ShapeDtypeStruct((rows, span), jnp.float32)] * n_col,
        in_specs=[HBM] * (n_row + 5),
        out_specs=[VMEM] * n_col,
        scratch_shapes=[
            pltpu.VMEM((n_col * rows, features), jnp.bfloat16),
            pltpu.VMEM((span, features), jnp.bfloat16),
            pltpu.SemaphoreType.DMA((2, n_row + 4)),
        ],
        compiler_params=TILE_PARAMS,
        cost_estimate=SHORT,
        name="tile_kernel",
    )(targets, support, mark, *near, *far)

    tiles = [made[0]] + [exchange(made[j], "col", n_col, j) for j in range(1, n_col)]
    tiles, blocks = together(tiles, blocks)
    corner = blocks[0, 0, :, :pivot].astype(jnp.float32) * (1 / PANEL_UNIT)
    head = tiles[0][:, :pivot]
    for j in range(1, n_col):
        head = jnp.where(col == j, tiles[j][:, :pivot], head)
    head = pl.pallas_call(
        head_kernel,
        out_shape=jax.ShapeDtypeStruct((rows, pivot), jnp.float32),
        in_specs=[VMEM] * 4,
        out_specs=VMEM,
        compiler_params=SOLVE_PARAMS,
        cost_estimate=SHORT,
        name="head_kernel",
    )(head, exchange(head, "row", n_row, 1), corner, diag_inverses)
    spread = head
    for i in range(2, n_row, 2):
        spread = jnp.where(row // 2 == i // 2, exchange(head, "row", n_row, i), spread)
    swapped = exchange(spread, "row", n_row, 1)
    blocks = blocks.astype(jnp.float32) * (1 / PANEL_UNIT)

    return pl.pallas_call(
        functools.partial(solve_kernel, n_col, pivot),
        out_shape=jax.ShapeDtypeStruct((rows, span * n_col), jnp.float32),
        in_specs=[VMEM] * (n_col + 4),
        out_specs=VMEM,
        compiler_params=SOLVE_PARAMS,
        name="solve_kernel",
    )(*tiles, panels, blocks, spread, swapped)


def solution(mesh):
    in_specs = (P(("row", "col"), None), P("col", None), P(None, None, ("row", "col")), P())
    body = functools.partial(shards, n_row=mesh.shape["row"], n_col=mesh.shape["col"])
    return jax.shard_map(body, mesh=mesh, in_specs=in_specs, out_specs=P("col", "row"), check_vma=False)
```

```python
import functools
import math

import jax
import jax.numpy as jnp
from jax import lax
from jax.experimental import pallas as pl
from jax.experimental.pallas import tpu as pltpu
from jax.sharding import PartitionSpec as P

VMEM = pl.BlockSpec(memory_space=pltpu.VMEM)
HBM = pl.BlockSpec(memory_space=pltpu.HBM)
TILE_PARAMS = pltpu.CompilerParams(vmem_limit_bytes=32 * 2**20)
SOLVE_PARAMS = pltpu.CompilerParams(vmem_limit_bytes=32 * 2**20)
LONG = pl.CostEstimate(flops=50_000_000_000, bytes_accessed=0, transcendentals=0)
SHORT = pl.CostEstimate(flops=1_000_000, bytes_accessed=0, transcendentals=0)
PANEL_UNIT = 2.0**17
NT = (((1,), (1,)), ((), ()))
TN = (((0,), (0,)), ((), ()))
NN = (((1,), (0,)), ((), ()))


def dot(a, b, dims):
    return lax.dot_general(a, b, dims, preferred_element_type=jnp.float32)


def halves(a):
    high = a.astype(jnp.bfloat16)
    return high, (a - high.astype(jnp.float32)).astype(jnp.bfloat16)


def dot32(a, b, dims):
    (a_high, a_low), (b_high, b_low) = halves(a), halves(b)
    return dot(a_high, b_high, dims) + (dot(a_low, b_high, dims) + dot(a_high, b_low, dims))


def start_all(pairs, sems):
    copies = [pltpu.make_async_copy(source, target, sems.at[i]) for i, (source, target) in enumerate(pairs)]
    for copy in copies:
        copy.start()
    return copies


def wait_all(copies):
    for copy in copies:
        copy.wait()


def cut_kernel(n_row, targets_hbm, mine_ref, half_ref, sems):
    row = lax.axis_index("row")
    (_, width), (_, half) = mine_ref.shape, half_ref.shape
    mine = pl.ds(pl.multiple_of((row // 2) * width, width), width)
    core = pl.ds(pl.multiple_of((row % 2) * half, half), half)
    wait_all(start_all([(targets_hbm.at[:, mine], mine_ref), (targets_hbm.at[:, core], half_ref)], sems))


def mark_kernel(value_ref, out_ref):
    out_ref[...] = value_ref[0, :8, :128]


def tile_kernel(scale, n_row, n_col, own_hbm, support_hbm, _, *refs):
    near, far, refs = refs[:2], refs[2:2 + n_row * (n_col // 2 - 1)], refs[2 + n_row * (n_col // 2 - 1):]
    outs, (targets_ref, support_ref, sems) = refs[:n_col], refs[n_col:]
    rows, features = own_hbm.shape
    row = lax.axis_index("row")
    chip, core = row // 2, row % 2
    half, width = features // 2, 2 * features // n_row
    steps = []
    for part in range(2):
        side = core ^ part
        cols = pl.ds(pl.multiple_of(side * half, half), half)
        loads = [
            (own_hbm.at[:, cols], targets_ref.at[pl.ds(0, rows), cols]),
            (support_hbm.at[:, cols], support_ref.at[:, cols]),
            (near[part], targets_ref.at[pl.ds(rows, rows), cols]),
        ]
        steps.append((cols, loads))
    loads = []
    for pair in range(n_col // 2 - 1):
        for step in range(n_row):
            plane = 2 * pair + 2 + (core ^ (step % 2))
            cols = pl.ds(pl.multiple_of((chip ^ (step // 2)) * width, width), width)
            spot = targets_ref.at[pl.ds(pl.multiple_of(plane * rows, rows), rows), cols]
            loads.append((far[pair * n_row + step], spot))
    steps[0][1].extend(loads)
    steps = [(cols, start_all(loads, sems.at[i])) for i, (cols, loads) in enumerate(steps)]
    total = 0.0
    for cols, copies in steps:
        wait_all(copies)
        total = total + dot(targets_ref[:, cols], support_ref[:, cols], NT)
    for plane in range(n_col):
        outs[plane][...] = jnp.exp(scale * total[plane * rows:(plane + 1) * rows])


def head_kernel(mine_ref, other_ref, corner_ref, inverse_ref, out_ref):
    odd = lax.axis_index("row") % 2
    other = jnp.where(odd == 1, other_ref[...], 0.0)
    head = mine_ref[...] - dot32(dot32(other, inverse_ref[0], NT), corner_ref[...], NN)
    out_ref[...] = dot32(head, inverse_ref[odd], NT)


def solve_kernel(n_col, pivot, *refs):
    tiles, (own_ref, panels_ref, mine_ref, other_ref, out_ref) = refs[:n_col], refs[n_col:]
    span = own_ref.shape[2]
    row, col = lax.axis_index("row"), lax.axis_index("col")
    even = row % 2 == 0
    mine, other = mine_ref[...], other_ref[...]
    first = jnp.where(even, mine, other)
    second = jnp.where(even, other, mine)
    for step in range(n_col):
        plane = col ^ step
        block = own_ref if step == 0 else panels_ref.at[plane]
        value = tiles[step][...] - dot32(first, block[0], NN) - dot32(second, block[1], NN)
        out_ref[:, pl.ds(pl.multiple_of(plane * span, span), span)] = value

    @pl.when(row == 0)
    def _():
        out_ref[:, :pivot] = first

    @pl.when(row == 1)
    def _():
        out_ref[:, :pivot] = second


def exchange(value, axis, size, mask):
    return lax.ppermute(value, axis, [(i, i ^ mask) for i in range(size)])


def together(*values):
    return lax.optimization_barrier(values)


def shards(support, targets, panels, diag_inverses, *, n_row, n_col):
    rows, features = targets.shape
    span = support.shape[0]
    pivot = diag_inverses.shape[1]
    scale = 0.5 / math.sqrt(features)
    row, col = lax.axis_index("row"), lax.axis_index("col")
    width = 2 * features // n_row

    mine, half = pl.pallas_call(
        functools.partial(cut_kernel, n_row),
        out_shape=[
            jax.ShapeDtypeStruct((rows, width), targets.dtype),
            jax.ShapeDtypeStruct((rows, features // 2), targets.dtype),
        ],
        in_specs=[HBM],
        out_specs=[VMEM] * 2,
        scratch_shapes=[pltpu.SemaphoreType.DMA((2,))],
        compiler_params=SOLVE_PARAMS,
        cost_estimate=SHORT,
        name="cut_kernel",
    )(targets)
    near = exchange(half, "col", n_col, 1)
    far = [
        lax.ppermute(mine, ("row", "col"), [
            (r * n_col + c, r * n_col + (c ^ (j + r % 2))) for r in range(n_row) for c in range(n_col)
        ])
        for j in range(2, n_col, 2)
    ]
    small = jnp.concatenate([panels * PANEL_UNIT] * n_col, axis=0).astype(jnp.float16)
    small = small.reshape(n_col, *panels.shape)
    blocks = lax.all_to_all(small, "col", 0, 0)
    mark = pl.pallas_call(
        mark_kernel,
        grid=(1,),
        out_shape=jax.ShapeDtypeStruct((8, 128), jnp.float32),
        in_specs=[pl.BlockSpec((1, 8, 128), lambda i: (0, 0, 0))],
        out_specs=VMEM,
        compiler_params=SOLVE_PARAMS,
        cost_estimate=LONG,
        name="mark_kernel",
    )(diag_inverses)
    far, mark = together(far, mark)
    near = [near, exchange(near, "row", n_row, 1)]
    pieces = []
    for own in far:
        for piece in [own] + [exchange(own, "row", n_row, i) for i in range(2, n_row, 2)]:
            pieces += [piece, exchange(piece, "row", n_row, 1)]

    made = pl.pallas_call(
        functools.partial(tile_kernel, scale, n_row, n_col),
        out_shape=[jax.ShapeDtypeStruct((rows, span), jnp.float32)] * n_col,
        in_specs=[HBM] * (len(pieces) + 5),
        out_specs=[VMEM] * n_col,
        scratch_shapes=[
            pltpu.VMEM((n_col * rows, features), jnp.bfloat16),
            pltpu.VMEM((span, features), jnp.bfloat16),
            pltpu.SemaphoreType.DMA((2, len(pieces) + 3)),
        ],
        compiler_params=TILE_PARAMS,
        cost_estimate=SHORT,
        name="tile_kernel",
    )(targets, support, mark, *near, *pieces)

    tiles = [made[0]] + [exchange(made[j], "col", n_col, j) for j in range(1, n_col)]
    tiles, blocks = together(tiles, blocks)
    corner = blocks[0, 0, :, :pivot].astype(jnp.float32) * (1 / PANEL_UNIT)
    head = tiles[0][:, :pivot]
    for j in range(1, n_col):
        head = jnp.where(col == j, tiles[j][:, :pivot], head)
    head = pl.pallas_call(
        head_kernel,
        out_shape=jax.ShapeDtypeStruct((rows, pivot), jnp.float32),
        in_specs=[VMEM] * 4,
        out_specs=VMEM,
        compiler_params=SOLVE_PARAMS,
        cost_estimate=SHORT,
        name="head_kernel",
    )(head, exchange(head, "row", n_row, 1), corner, diag_inverses)
    spread = head
    for i in range(2, n_row, 2):
        spread = jnp.where(row // 2 == i // 2, exchange(head, "row", n_row, i), spread)
    swapped = exchange(spread, "row", n_row, 1)
    blocks = blocks.astype(jnp.float32) * (1 / PANEL_UNIT)

    return pl.pallas_call(
        functools.partial(solve_kernel, n_col, pivot),
        out_shape=jax.ShapeDtypeStruct((rows, span * n_col), jnp.float32),
        in_specs=[VMEM] * (n_col + 4),
        out_specs=VMEM,
        compiler_params=SOLVE_PARAMS,
        name="solve_kernel",
    )(*tiles, panels, blocks, spread, swapped)


def solution(mesh):
    in_specs = (P(("row", "col"), None), P("col", None), P(None, None, ("row", "col")), P())
    body = functools.partial(shards, n_row=mesh.shape["row"], n_col=mesh.shape["col"])
    return jax.shard_map(body, mesh=mesh, in_specs=in_specs, out_specs=P("col", "row"), check_vma=False)
```

```python
import functools
import math

import jax
import jax.numpy as jnp
from jax import lax
from jax.experimental import pallas as pl
from jax.experimental.pallas import tpu as pltpu
from jax.sharding import PartitionSpec as P

VMEM = pl.BlockSpec(memory_space=pltpu.VMEM)
HBM = pl.BlockSpec(memory_space=pltpu.HBM)
TILE_PARAMS = pltpu.CompilerParams(vmem_limit_bytes=32 * 2**20)
SOLVE_PARAMS = pltpu.CompilerParams(vmem_limit_bytes=32 * 2**20)
LONG = pl.CostEstimate(flops=50_000_000_000, bytes_accessed=0, transcendentals=0)
SHORT = pl.CostEstimate(flops=1_000_000, bytes_accessed=0, transcendentals=0)
PANEL_UNIT = 2.0**17
NT = (((1,), (1,)), ((), ()))
TN = (((0,), (0,)), ((), ()))
NN = (((1,), (0,)), ((), ()))


def dot(a, b, dims):
    return lax.dot_general(a, b, dims, preferred_element_type=jnp.float32)


def halves(a):
    high = a.astype(jnp.bfloat16)
    return high, (a - high.astype(jnp.float32)).astype(jnp.bfloat16)


def dot32(a, b, dims):
    (a_high, a_low), (b_high, b_low) = halves(a), halves(b)
    return dot(a_high, b_high, dims) + (dot(a_low, b_high, dims) + dot(a_high, b_low, dims))


def start_all(pairs, sems):
    copies = [pltpu.make_async_copy(source, target, sems.at[i]) for i, (source, target) in enumerate(pairs)]
    for copy in copies:
        copy.start()
    return copies


def wait_all(copies):
    for copy in copies:
        copy.wait()


def cut_kernel(n_row, targets_hbm, mine_ref, half_ref, sems):
    row = lax.axis_index("row")
    (_, width), (_, half) = mine_ref.shape, half_ref.shape
    mine = pl.ds(pl.multiple_of((row // 2) * width, width), width)
    core = pl.ds(pl.multiple_of((row % 2) * half, half), half)
    wait_all(start_all([(targets_hbm.at[:, mine], mine_ref), (targets_hbm.at[:, core], half_ref)], sems))


def mark_kernel(value_ref, out_ref):
    out_ref[...] = value_ref[0, :8, :128]


def tile_kernel(scale, n_row, n_col, own_hbm, support_ref, _, *refs):
    near, far, refs = refs[:2], refs[2:2 + n_row * (n_col // 2 - 1)], refs[2 + n_row * (n_col // 2 - 1):]
    outs, (targets_ref, sems) = refs[:n_col + 1], refs[n_col + 1:]
    rows, features = own_hbm.shape
    row = lax.axis_index("row")
    chip, core = row // 2, row % 2
    half, width = features // 2, 2 * features // n_row
    steps = []
    for part in range(2):
        side = core ^ part
        cols = pl.ds(pl.multiple_of(side * half, half), half)
        loads = [
            (own_hbm.at[:, cols], targets_ref.at[pl.ds(0, rows), cols]),
            (near[part], targets_ref.at[pl.ds(rows, rows), cols]),
        ]
        steps.append((cols, loads))
    loads = []
    for pair in range(n_col // 2 - 1):
        for step in range(n_row):
            plane = 2 * pair + 2 + (core ^ (step % 2))
            cols = pl.ds(pl.multiple_of((chip ^ (step // 2)) * width, width), width)
            spot = targets_ref.at[pl.ds(pl.multiple_of(plane * rows, rows), rows), cols]
            loads.append((far[pair * n_row + step], spot))
    steps[0][1].extend(loads)
    steps = [(cols, start_all(loads, sems.at[i])) for i, (cols, loads) in enumerate(steps)]
    total = 0.0
    for cols, copies in steps:
        wait_all(copies)
        total = total + dot(targets_ref[:, cols], support_ref[:, cols], NT)
    starts = [0, rows, rows + rows // 2, *range(2 * rows, n_col * rows, rows)]
    for start, out_ref in zip(starts, outs):
        out_ref[...] = jnp.exp(scale * total[start:start + out_ref.shape[0]])


def head_kernel(mine_ref, other_ref, corner_ref, inverse_ref, out_ref):
    odd = lax.axis_index("row") % 2
    other = jnp.where(odd == 1, other_ref[...], 0.0)
    head = mine_ref[...] - dot32(dot32(other, inverse_ref[0], NT), corner_ref[...], NN)
    out_ref[...] = dot32(head, inverse_ref[odd], NT)


def solve_kernel(n_col, pivot, *refs):
    tiles, refs = [ref[...] for ref in refs[:n_col + 1]], refs[n_col + 1:]
    tiles[1:3] = [jnp.concatenate(tiles[1:3], axis=0)]
    own_ref, panels_ref, mine_ref, other_ref, out_ref = refs
    span = own_ref.shape[2]
    row, col = lax.axis_index("row"), lax.axis_index("col")
    even = row % 2 == 0
    mine, other = mine_ref[...], other_ref[...]
    first = jnp.where(even, mine, other)
    second = jnp.where(even, other, mine)
    for step in range(n_col):
        plane = col ^ step
        block = own_ref if step == 0 else panels_ref.at[plane]
        value = tiles[step] - dot32(first, block[0], NN) - dot32(second, block[1], NN)
        out_ref[:, pl.ds(pl.multiple_of(plane * span, span), span)] = value

    @pl.when(row == 0)
    def _():
        out_ref[:, :pivot] = first

    @pl.when(row == 1)
    def _():
        out_ref[:, :pivot] = second


def exchange(value, axis, size, mask):
    return lax.ppermute(value, axis, [(i, i ^ mask) for i in range(size)])


def together(*values):
    return lax.optimization_barrier(values)


def shards(support, targets, panels, diag_inverses, *, n_row, n_col):
    rows, features = targets.shape
    span = support.shape[0]
    pivot = diag_inverses.shape[1]
    scale = 0.5 / math.sqrt(features)
    row, col = lax.axis_index("row"), lax.axis_index("col")
    width = 2 * features // n_row

    mine, half = pl.pallas_call(
        functools.partial(cut_kernel, n_row),
        out_shape=[
            jax.ShapeDtypeStruct((rows, width), targets.dtype),
            jax.ShapeDtypeStruct((rows, features // 2), targets.dtype),
        ],
        in_specs=[HBM],
        out_specs=[VMEM] * 2,
        scratch_shapes=[pltpu.SemaphoreType.DMA((2,))],
        compiler_params=SOLVE_PARAMS,
        cost_estimate=SHORT,
        name="cut_kernel",
    )(targets)
    near = exchange(half, "col", n_col, 1)
    far = [
        lax.ppermute(mine, ("row", "col"), [
            (r * n_col + c, r * n_col + (c ^ (j + r % 2))) for r in range(n_row) for c in range(n_col)
        ])
        for j in range(2, n_col, 2)
    ]
    small = jnp.concatenate([panels * PANEL_UNIT] * n_col, axis=0).astype(jnp.float16)
    small = small.reshape(n_col, *panels.shape)
    blocks = lax.all_to_all(small, "col", 0, 0)
    mark = pl.pallas_call(
        mark_kernel,
        grid=(1,),
        out_shape=jax.ShapeDtypeStruct((8, 128), jnp.float32),
        in_specs=[pl.BlockSpec((1, 8, 128), lambda i: (0, 0, 0))],
        out_specs=VMEM,
        compiler_params=SOLVE_PARAMS,
        cost_estimate=LONG,
        name="mark_kernel",
    )(diag_inverses)
    far, mark = together(far, mark)
    near = [near, exchange(near, "row", n_row, 1)]
    pieces = []
    for own in far:
        for piece in [own] + [exchange(own, "row", n_row, i) for i in range(2, n_row, 2)]:
            pieces += [piece, exchange(piece, "row", n_row, 1)]

    made = pl.pallas_call(
        functools.partial(tile_kernel, scale, n_row, n_col),
        out_shape=[
            jax.ShapeDtypeStruct((count, span), jnp.float32)
            for count in [rows, rows // 2, rows // 2] + [rows] * (n_col - 2)
        ],
        in_specs=[HBM, VMEM] + [HBM] * (len(pieces) + 3),
        out_specs=[VMEM] * (n_col + 1),
        scratch_shapes=[
            pltpu.VMEM((n_col * rows, features), jnp.bfloat16),
            pltpu.SemaphoreType.DMA((2, len(pieces) + 3)),
        ],
        compiler_params=TILE_PARAMS,
        cost_estimate=SHORT,
        name="tile_kernel",
    )(targets, support, mark, *near, *pieces)

    tiles = [made[0]] + [exchange(made[i], "col", n_col, max(1, i - 1)) for i in range(1, n_col + 1)]
    tiles, blocks = together(tiles, blocks)
    corner = blocks[0, 0, :, :pivot].astype(jnp.float32) * (1 / PANEL_UNIT)
    heads = [tile[:, :pivot] for tile in tiles]
    heads[1:3] = [jnp.concatenate(heads[1:3], axis=0)]
    head = heads[0]
    for j in range(1, n_col):
        head = jnp.where(col == j, heads[j], head)
    head = pl.pallas_call(
        head_kernel,
        out_shape=jax.ShapeDtypeStruct((rows, pivot), jnp.float32),
        in_specs=[VMEM] * 4,
        out_specs=VMEM,
        compiler_params=SOLVE_PARAMS,
        cost_estimate=SHORT,
        name="head_kernel",
    )(head, exchange(head, "row", n_row, 1), corner, diag_inverses)
    spread = head
    for i in range(2, n_row, 2):
        spread = jnp.where(row // 2 == i // 2, exchange(head, "row", n_row, i), spread)
    swapped = exchange(spread, "row", n_row, 1)
    blocks = blocks.astype(jnp.float32) * (1 / PANEL_UNIT)

    return pl.pallas_call(
        functools.partial(solve_kernel, n_col, pivot),
        out_shape=jax.ShapeDtypeStruct((rows, span * n_col), jnp.float32),
        in_specs=[VMEM] * (n_col + 5),
        out_specs=VMEM,
        compiler_params=SOLVE_PARAMS,
        name="solve_kernel",
    )(*tiles, panels, blocks, spread, swapped)


def solution(mesh):
    in_specs = (P(("row", "col"), None), P("col", None), P(None, None, ("row", "col")), P())
    body = functools.partial(shards, n_row=mesh.shape["row"], n_col=mesh.shape["col"])
    return jax.shard_map(body, mesh=mesh, in_specs=in_specs, out_specs=P("col", "row"), check_vma=False)
```

```python
import functools
import math

import jax
import jax.numpy as jnp
from jax import lax
from jax.experimental import pallas as pl
from jax.experimental.pallas import tpu as pltpu
from jax.sharding import PartitionSpec as P

VMEM = pl.BlockSpec(memory_space=pltpu.VMEM)
HBM = pl.BlockSpec(memory_space=pltpu.HBM)
TILE_PARAMS = pltpu.CompilerParams(vmem_limit_bytes=32 * 2**20)
SOLVE_PARAMS = pltpu.CompilerParams(vmem_limit_bytes=32 * 2**20)
LONG = pl.CostEstimate(flops=50_000_000_000, bytes_accessed=0, transcendentals=0)
SHORT = pl.CostEstimate(flops=1_000_000, bytes_accessed=0, transcendentals=0)
PANEL_UNIT = 2.0**17
NT = (((1,), (1,)), ((), ()))
TN = (((0,), (0,)), ((), ()))
NN = (((1,), (0,)), ((), ()))


def dot(a, b, dims):
    return lax.dot_general(a, b, dims, preferred_element_type=jnp.float32)


def halves(a):
    high = a.astype(jnp.bfloat16)
    return high, (a - high.astype(jnp.float32)).astype(jnp.bfloat16)


def dot32(a, b, dims):
    (a_high, a_low), (b_high, b_low) = halves(a), halves(b)
    return dot(a_high, b_high, dims) + (dot(a_low, b_high, dims) + dot(a_high, b_low, dims))


def start_all(pairs, sems):
    copies = [pltpu.make_async_copy(source, target, sems.at[i]) for i, (source, target) in enumerate(pairs)]
    for copy in copies:
        copy.start()
    return copies


def wait_all(copies):
    for copy in copies:
        copy.wait()


def cut_kernel(n_row, targets_hbm, mine_ref, half_ref, sems):
    row = lax.axis_index("row")
    (_, width), (_, half) = mine_ref.shape, half_ref.shape
    mine = pl.ds(pl.multiple_of((row // 2) * width, width), width)
    core = pl.ds(pl.multiple_of((row % 2) * half, half), half)
    wait_all(start_all([(targets_hbm.at[:, mine], mine_ref), (targets_hbm.at[:, core], half_ref)], sems))


def mark_kernel(value_ref, out_ref):
    out_ref[...] = value_ref[0, :8, :128]


def tile_kernel(scale, n_row, n_col, own_hbm, support_ref, _, *refs):
    near, far, refs = refs[:2], refs[2:2 + n_row * (n_col // 2 - 1)], refs[2 + n_row * (n_col // 2 - 1):]
    outs, (targets_ref, sems) = refs[:n_col + 1], refs[n_col + 1:]
    rows, features = own_hbm.shape
    row = lax.axis_index("row")
    chip, core = row // 2, row % 2
    half, width = features // 2, 2 * features // n_row
    steps = []
    for part in range(2):
        side = core ^ part
        cols = pl.ds(pl.multiple_of(side * half, half), half)
        loads = [
            (own_hbm.at[:, cols], targets_ref.at[pl.ds(0, rows), cols]),
            (near[part], targets_ref.at[pl.ds(rows, rows), cols]),
        ]
        steps.append((cols, loads))
    loads = []
    for pair in range(n_col // 2 - 1):
        for step in range(n_row):
            plane = 2 * pair + 2 + (core ^ (step % 2))
            cols = pl.ds(pl.multiple_of((chip ^ (step // 2)) * width, width), width)
            spot = targets_ref.at[pl.ds(pl.multiple_of(plane * rows, rows), rows), cols]
            loads.append((far[pair * n_row + step], spot))
    steps[0][1].extend(loads)
    steps = [(cols, start_all(loads, sems.at[i])) for i, (cols, loads) in enumerate(steps)]
    total = 0.0
    for cols, copies in steps:
        wait_all(copies)
        total = total + dot(targets_ref[:, cols], support_ref[:, cols], NT)
    starts = [0, rows, rows + rows // 2, *range(2 * rows, n_col * rows, rows)]
    for start, out_ref in zip(starts, outs):
        out_ref[...] = jnp.exp(scale * total[start:start + out_ref.shape[0]])


def mix_kernel(corner_ref, inverse_ref, out_ref):
    out_ref[...] = dot32(dot32(inverse_ref[0], corner_ref[...], TN), inverse_ref[1], NT)


def base_kernel(mine_ref, inverse_ref, out_ref):
    out_ref[...] = dot32(mine_ref[...], inverse_ref[lax.axis_index("row") % 2], NT)


def head_kernel(base_ref, other_ref, mix_ref, out_ref):
    other = jnp.where(lax.axis_index("row") % 2 == 1, other_ref[...], 0.0)
    out_ref[...] = base_ref[...] - dot32(other, mix_ref[...], NN)


def mine_kernel(n_col, *refs):
    tiles, refs = [ref[...] for ref in refs[:n_col + 1]], refs[n_col + 1:]
    tiles[1:3] = [jnp.concatenate(tiles[1:3], axis=0)]
    own_ref, panels_ref, mine_ref, out_ref = refs
    span = own_ref.shape[2]
    row, col = lax.axis_index("row"), lax.axis_index("col")
    for step in range(n_col):
        plane = col ^ step
        block = own_ref if step == 0 else panels_ref.at[plane]
        value = tiles[step] - dot32(mine_ref[...], block[row % 2], NN)
        out_ref[:, pl.ds(pl.multiple_of(plane * span, span), span)] = value


def other_kernel(n_col, pivot, part_ref, own_ref, panels_ref, mine_ref, other_ref, out_ref):
    span = own_ref.shape[2]
    row, col = lax.axis_index("row"), lax.axis_index("col")
    for step in range(n_col):
        plane = col ^ step
        block = own_ref if step == 0 else panels_ref.at[plane]
        cols = pl.ds(pl.multiple_of(plane * span, span), span)
        out_ref[:, cols] = part_ref[:, cols] - dot32(other_ref[...], block[1 - row % 2], NN)

    @pl.when(row < 2)
    def _():
        out_ref[:, :pivot] = mine_ref[...]


def exchange(value, axis, size, mask):
    return lax.ppermute(value, axis, [(i, i ^ mask) for i in range(size)])


def together(*values):
    return lax.optimization_barrier(values)


def shards(support, targets, panels, diag_inverses, *, n_row, n_col):
    rows, features = targets.shape
    span = support.shape[0]
    pivot = diag_inverses.shape[1]
    scale = 0.5 / math.sqrt(features)
    row, col = lax.axis_index("row"), lax.axis_index("col")
    width = 2 * features // n_row

    mine, half = pl.pallas_call(
        functools.partial(cut_kernel, n_row),
        out_shape=[
            jax.ShapeDtypeStruct((rows, width), targets.dtype),
            jax.ShapeDtypeStruct((rows, features // 2), targets.dtype),
        ],
        in_specs=[HBM],
        out_specs=[VMEM] * 2,
        scratch_shapes=[pltpu.SemaphoreType.DMA((2,))],
        compiler_params=SOLVE_PARAMS,
        cost_estimate=SHORT,
        name="cut_kernel",
    )(targets)
    near = exchange(half, "col", n_col, 1)
    far = [
        lax.ppermute(mine, ("row", "col"), [
            (r * n_col + c, r * n_col + (c ^ (j + r % 2))) for r in range(n_row) for c in range(n_col)
        ])
        for j in range(2, n_col, 2)
    ]
    small = jnp.concatenate([panels * PANEL_UNIT] * n_col, axis=0).astype(jnp.float16)
    small = small.reshape(n_col, *panels.shape)
    blocks = lax.all_to_all(small, "col", 0, 0)
    mark = pl.pallas_call(
        mark_kernel,
        grid=(1,),
        out_shape=jax.ShapeDtypeStruct((8, 128), jnp.float32),
        in_specs=[pl.BlockSpec((1, 8, 128), lambda i: (0, 0, 0))],
        out_specs=VMEM,
        compiler_params=SOLVE_PARAMS,
        cost_estimate=LONG,
        name="mark_kernel",
    )(diag_inverses)
    far, mark = together(far, mark)
    near = [near, exchange(near, "row", n_row, 1)]
    pieces = []
    for own in far:
        for piece in [own] + [exchange(own, "row", n_row, i) for i in range(2, n_row, 2)]:
            pieces += [piece, exchange(piece, "row", n_row, 1)]

    made = pl.pallas_call(
        functools.partial(tile_kernel, scale, n_row, n_col),
        out_shape=[
            jax.ShapeDtypeStruct((count, span), jnp.float32)
            for count in [rows, rows // 2, rows // 2] + [rows] * (n_col - 2)
        ],
        in_specs=[HBM, VMEM] + [HBM] * (len(pieces) + 3),
        out_specs=[VMEM] * (n_col + 1),
        scratch_shapes=[
            pltpu.VMEM((n_col * rows, features), jnp.bfloat16),
            pltpu.SemaphoreType.DMA((2, len(pieces) + 3)),
        ],
        compiler_params=TILE_PARAMS,
        cost_estimate=SHORT,
        name="tile_kernel",
    )(targets, support, mark, *near, *pieces)

    tiles = [made[0]] + [exchange(made[i], "col", n_col, max(1, i - 1)) for i in range(1, n_col + 1)]
    tiles, blocks = together(tiles, blocks)
    corner = blocks[0, 0, :, :pivot].astype(jnp.float32) * (1 / PANEL_UNIT)
    heads = [tile[:, :pivot] for tile in tiles]
    heads[1:3] = [jnp.concatenate(heads[1:3], axis=0)]
    head = heads[0]
    for j in range(1, n_col):
        head = jnp.where(col == j, heads[j], head)
    mix = pl.pallas_call(
        mix_kernel,
        out_shape=jax.ShapeDtypeStruct((pivot, pivot), jnp.float32),
        in_specs=[VMEM] * 2,
        out_specs=VMEM,
        compiler_params=SOLVE_PARAMS,
        cost_estimate=SHORT,
        name="mix_kernel",
    )(corner, diag_inverses)
    base = pl.pallas_call(
        base_kernel,
        out_shape=jax.ShapeDtypeStruct((rows, pivot), jnp.float32),
        in_specs=[VMEM] * 2,
        out_specs=VMEM,
        compiler_params=SOLVE_PARAMS,
        cost_estimate=SHORT,
        name="base_kernel",
    )(head, diag_inverses)
    head = pl.pallas_call(
        head_kernel,
        out_shape=jax.ShapeDtypeStruct((rows, pivot), jnp.float32),
        in_specs=[VMEM] * 3,
        out_specs=VMEM,
        compiler_params=SOLVE_PARAMS,
        cost_estimate=SHORT,
        name="head_kernel",
    )(base, exchange(head, "row", n_row, 1), mix)
    spread = head
    for i in range(2, n_row, 2):
        spread = jnp.where(row // 2 == i // 2, exchange(head, "row", n_row, i), spread)
    swapped = exchange(spread, "row", n_row, 1)
    blocks = blocks.astype(jnp.float32) * (1 / PANEL_UNIT)

    part = pl.pallas_call(
        functools.partial(mine_kernel, n_col),
        out_shape=jax.ShapeDtypeStruct((rows, span * n_col), jnp.float32),
        in_specs=[VMEM] * (n_col + 4),
        out_specs=VMEM,
        compiler_params=SOLVE_PARAMS,
        cost_estimate=SHORT,
        name="mine_kernel",
    )(*tiles, panels, blocks, spread)
    return pl.pallas_call(
        functools.partial(other_kernel, n_col, pivot),
        out_shape=jax.ShapeDtypeStruct((rows, span * n_col), jnp.float32),
        in_specs=[VMEM] * 5,
        out_specs=VMEM,
        compiler_params=SOLVE_PARAMS,
        cost_estimate=SHORT,
        name="other_kernel",
    )(part, panels, blocks, spread, swapped)


def solution(mesh):
    in_specs = (P(("row", "col"), None), P("col", None), P(None, None, ("row", "col")), P())
    body = functools.partial(shards, n_row=mesh.shape["row"], n_col=mesh.shape["col"])
    return jax.shard_map(body, mesh=mesh, in_specs=in_specs, out_specs=P("col", "row"), check_vma=False)
```

```python
import functools
import math

import jax
import jax.numpy as jnp
from jax import lax
from jax.experimental import pallas as pl
from jax.experimental.pallas import tpu as pltpu
from jax.sharding import PartitionSpec as P

VMEM = pl.BlockSpec(memory_space=pltpu.VMEM)
HBM = pl.BlockSpec(memory_space=pltpu.HBM)
TILE_PARAMS = pltpu.CompilerParams(vmem_limit_bytes=32 * 2**20)
SOLVE_PARAMS = pltpu.CompilerParams(vmem_limit_bytes=32 * 2**20)
LONG = pl.CostEstimate(flops=50_000_000_000, bytes_accessed=0, transcendentals=0)
SHORT = pl.CostEstimate(flops=1_000_000, bytes_accessed=0, transcendentals=0)
PANEL_UNIT = 2.0**17
NT = (((1,), (1,)), ((), ()))
TN = (((0,), (0,)), ((), ()))
NN = (((1,), (0,)), ((), ()))


def dot(a, b, dims):
    return lax.dot_general(a, b, dims, preferred_element_type=jnp.float32)


def halves(a):
    high = a.astype(jnp.bfloat16)
    return high, (a - high.astype(jnp.float32)).astype(jnp.bfloat16)


def dot32(a, b, dims):
    (a_high, a_low), (b_high, b_low) = halves(a), halves(b)
    return dot(a_high, b_high, dims) + (dot(a_low, b_high, dims) + dot(a_high, b_low, dims))


def start_all(pairs, sems):
    copies = [pltpu.make_async_copy(source, target, sems.at[i]) for i, (source, target) in enumerate(pairs)]
    for copy in copies:
        copy.start()
    return copies


def wait_all(copies):
    for copy in copies:
        copy.wait()


def cut_kernel(n_row, targets_hbm, mine_ref, half_ref, sems):
    row = lax.axis_index("row")
    (_, width), (_, half) = mine_ref.shape, half_ref.shape
    mine = pl.ds(pl.multiple_of((row // 2) * width, width), width)
    core = pl.ds(pl.multiple_of((row % 2) * half, half), half)
    wait_all(start_all([(targets_hbm.at[:, mine], mine_ref), (targets_hbm.at[:, core], half_ref)], sems))


def mark_kernel(value_ref, out_ref):
    out_ref[...] = value_ref[0, :8, :128]


def mine_tile_kernel(scale, n_row, own_hbm, support_ref, _, *refs):
    planes = (len(refs) - 3) // (n_row // 2 + 1)
    far, outs, (targets_ref, sems) = refs[:-3 - planes], refs[-3 - planes:-2], refs[-2:]
    rows = own_hbm.shape[0]
    loads = [(own_hbm, targets_ref.at[pl.ds(0, rows)])] + far_loads(n_row, rows, far, targets_ref, 1)
    wait_all(start_all(loads, sems))
    kernel = jnp.exp(scale * dot(targets_ref[...], support_ref[...], NT))
    for plane, out_ref in enumerate(outs):
        out_ref[...] = kernel[plane * rows:(plane + 1) * rows]


def far_loads(n_row, rows, far, targets_ref, first):
    chip, width = lax.axis_index("row") // 2, far[0].shape[1]
    loads = []
    for i, piece in enumerate(far):
        plane, step = divmod(i, n_row // 2)
        cols = pl.ds(pl.multiple_of((chip ^ step) * width, width), width)
        loads.append((piece, targets_ref.at[pl.ds((first + plane) * rows, rows), cols]))
    return loads


def other_tile_kernel(scale, n_row, support_ref, *refs):
    planes = (len(refs) - 6) // (n_row // 2 + 1)
    near, far, refs = refs[:2], refs[2:-4 - planes], refs[-4 - planes:]
    outs, (targets_ref, sems) = refs[:-2], refs[-2:]
    rows, half = near[0].shape
    row = lax.axis_index("row")
    loads = far_loads(n_row, rows, far, targets_ref, 1)
    for part in range(2):
        cols = pl.ds(pl.multiple_of((row % 2 ^ part) * half, half), half)
        loads.append((near[part], targets_ref.at[pl.ds(0, rows), cols]))
    wait_all(start_all(loads, sems))
    kernel = jnp.exp(scale * dot(targets_ref[...], support_ref[...], NT))
    starts = [0, rows // 2, *range(rows, targets_ref.shape[0], rows)]
    for start, out_ref in zip(starts, outs):
        out_ref[...] = kernel[start:start + out_ref.shape[0]]


def plane_offsets(n_col, core):
    return [0, 1] + [2 * pair + 2 + core for pair in range(n_col // 2 - 1)] + [
        2 * pair + 3 - core for pair in range(n_col // 2 - 1)
    ]


def mix_kernel(corner_ref, inverse_ref, out_ref):
    out_ref[...] = dot32(dot32(inverse_ref[0], corner_ref[...], TN), inverse_ref[1], NT)


def base_kernel(mine_ref, inverse_ref, out_ref):
    out_ref[...] = dot32(mine_ref[...], inverse_ref[lax.axis_index("row") % 2], NT)


def head_kernel(base_ref, other_ref, mix_ref, out_ref):
    other = jnp.where(lax.axis_index("row") % 2 == 1, other_ref[...], 0.0)
    out_ref[...] = base_ref[...] - dot32(other, mix_ref[...], NN)


def mine_kernel(n_col, *refs):
    tiles, refs = [ref[...] for ref in refs[:n_col + 1]], refs[n_col + 1:]
    tiles[1:3] = [jnp.concatenate(tiles[1:3], axis=0)]
    own_ref, panels_ref, mine_ref, out_ref = refs
    span = own_ref.shape[2]
    row, col = lax.axis_index("row"), lax.axis_index("col")
    for step, offset in enumerate(plane_offsets(n_col, row % 2)):
        plane = col ^ offset
        block = own_ref if step == 0 else panels_ref.at[plane]
        value = tiles[step] - dot32(mine_ref[...], block[row % 2], NN)
        out_ref[:, pl.ds(pl.multiple_of(plane * span, span), span)] = value


def other_kernel(n_col, pivot, part_ref, own_ref, panels_ref, mine_ref, other_ref, out_ref):
    span = own_ref.shape[2]
    row, col = lax.axis_index("row"), lax.axis_index("col")
    for step in range(n_col):
        plane = col ^ step
        block = own_ref if step == 0 else panels_ref.at[plane]
        cols = pl.ds(pl.multiple_of(plane * span, span), span)
        out_ref[:, cols] = part_ref[:, cols] - dot32(other_ref[...], block[1 - row % 2], NN)

    @pl.when(row < 2)
    def _():
        out_ref[:, :pivot] = mine_ref[...]


def exchange(value, axis, size, mask):
    return lax.ppermute(value, axis, [(i, i ^ mask) for i in range(size)])


def together(*values):
    return lax.optimization_barrier(values)


def shards(support, targets, panels, diag_inverses, *, n_row, n_col):
    rows, features = targets.shape
    span = support.shape[0]
    pivot = diag_inverses.shape[1]
    scale = 0.5 / math.sqrt(features)
    row, col = lax.axis_index("row"), lax.axis_index("col")
    width = 2 * features // n_row

    mine, half = pl.pallas_call(
        functools.partial(cut_kernel, n_row),
        out_shape=[
            jax.ShapeDtypeStruct((rows, width), targets.dtype),
            jax.ShapeDtypeStruct((rows, features // 2), targets.dtype),
        ],
        in_specs=[HBM],
        out_specs=[VMEM] * 2,
        scratch_shapes=[pltpu.SemaphoreType.DMA((2,))],
        compiler_params=SOLVE_PARAMS,
        cost_estimate=SHORT,
        name="cut_kernel",
    )(targets)
    near = exchange(half, "col", n_col, 1)
    far = [
        lax.ppermute(mine, ("row", "col"), [
            (r * n_col + c, r * n_col + (c ^ (j + r % 2))) for r in range(n_row) for c in range(n_col)
        ])
        for j in range(2, n_col, 2)
    ]
    small = jnp.concatenate([panels * PANEL_UNIT] * n_col, axis=0).astype(jnp.float16)
    small = small.reshape(n_col, *panels.shape)
    blocks = lax.all_to_all(small, "col", 0, 0)
    mark = pl.pallas_call(
        mark_kernel,
        grid=(1,),
        out_shape=jax.ShapeDtypeStruct((8, 128), jnp.float32),
        in_specs=[pl.BlockSpec((1, 8, 128), lambda i: (0, 0, 0))],
        out_specs=VMEM,
        compiler_params=SOLVE_PARAMS,
        cost_estimate=LONG,
        name="mark_kernel",
    )(diag_inverses)
    far, mark = together(far, mark)
    near = [near, exchange(near, "row", n_row, 1)]
    mine_far = [
        piece for own in far for piece in [own] + [exchange(own, "row", n_row, i) for i in range(2, n_row, 2)]
    ]
    other_far = [exchange(piece, "row", n_row, 1) for piece in mine_far]

    def tile_call(body, name, counts, *operands):
        pieces = len(operands) - 1
        return list(pl.pallas_call(
            functools.partial(body, scale, n_row),
            out_shape=[jax.ShapeDtypeStruct((count, span), jnp.float32) for count in counts],
            in_specs=[VMEM if operand is support else HBM for operand in operands],
            out_specs=[VMEM] * len(counts),
            scratch_shapes=[
                pltpu.VMEM(((1 + len(far)) * rows, features), jnp.bfloat16),
                pltpu.SemaphoreType.DMA((pieces,)),
            ],
            compiler_params=TILE_PARAMS,
            cost_estimate=SHORT,
            name=name,
        )(*operands))

    first = tile_call(
        mine_tile_kernel, "mine_tile_kernel", [rows] * (1 + len(far)), targets, support, mark, *mine_far
    )
    first[0], *other_far = together(first[0], *other_far)
    last = tile_call(
        other_tile_kernel, "other_tile_kernel", [rows // 2] * 2 + [rows] * len(far), support, *near, *other_far
    )
    made = [first[0], *last[:2], *first[1:], *last[2:]]

    tiles = [made[0]] + [exchange(tile, "col", n_col, 1) for tile in made[1:3]]
    for i, tile in enumerate(made[3:]):
        turn, pair = divmod(i, len(far))
        tiles.append(lax.ppermute(tile, ("row", "col"), [
            (r * n_col + c, r * n_col + (c ^ (2 * pair + 2 + (r + turn) % 2))) for r in range(n_row) for c in range(n_col)
        ]))
    tiles, blocks = together(tiles, blocks)
    corner = blocks[0, 0, :, :pivot].astype(jnp.float32) * (1 / PANEL_UNIT)
    heads = [tile[:, :pivot] for tile in tiles]
    heads[1:3] = [jnp.concatenate(heads[1:3], axis=0)]
    head = heads[0]
    for offset, value in zip(plane_offsets(n_col, row % 2)[1:], heads[1:]):
        head = jnp.where(col == offset, value, head)
    mix = pl.pallas_call(
        mix_kernel,
        out_shape=jax.ShapeDtypeStruct((pivot, pivot), jnp.float32),
        in_specs=[VMEM] * 2,
        out_specs=VMEM,
        compiler_params=SOLVE_PARAMS,
        cost_estimate=SHORT,
        name="mix_kernel",
    )(corner, diag_inverses)
    base = pl.pallas_call(
        base_kernel,
        out_shape=jax.ShapeDtypeStruct((rows, pivot), jnp.float32),
        in_specs=[VMEM] * 2,
        out_specs=VMEM,
        compiler_params=SOLVE_PARAMS,
        cost_estimate=SHORT,
        name="base_kernel",
    )(head, diag_inverses)
    head = pl.pallas_call(
        head_kernel,
        out_shape=jax.ShapeDtypeStruct((rows, pivot), jnp.float32),
        in_specs=[VMEM] * 3,
        out_specs=VMEM,
        compiler_params=SOLVE_PARAMS,
        cost_estimate=SHORT,
        name="head_kernel",
    )(base, exchange(head, "row", n_row, 1), mix)
    spread = head
    for i in range(2, n_row, 2):
        spread = jnp.where(row // 2 == i // 2, exchange(head, "row", n_row, i), spread)
    swapped = exchange(spread, "row", n_row, 1)
    blocks = blocks.astype(jnp.float32) * (1 / PANEL_UNIT)

    part = pl.pallas_call(
        functools.partial(mine_kernel, n_col),
        out_shape=jax.ShapeDtypeStruct((rows, span * n_col), jnp.float32),
        in_specs=[VMEM] * (n_col + 4),
        out_specs=VMEM,
        compiler_params=SOLVE_PARAMS,
        cost_estimate=SHORT,
        name="mine_kernel",
    )(*tiles, panels, blocks, spread)
    return pl.pallas_call(
        functools.partial(other_kernel, n_col, pivot),
        out_shape=jax.ShapeDtypeStruct((rows, span * n_col), jnp.float32),
        in_specs=[VMEM] * 5,
        out_specs=VMEM,
        compiler_params=SOLVE_PARAMS,
        cost_estimate=SHORT,
        name="other_kernel",
    )(part, panels, blocks, spread, swapped)


def solution(mesh):
    in_specs = (P(("row", "col"), None), P("col", None), P(None, None, ("row", "col")), P())
    body = functools.partial(shards, n_row=mesh.shape["row"], n_col=mesh.shape["col"])
    return jax.shard_map(body, mesh=mesh, in_specs=in_specs, out_specs=P("col", "row"), check_vma=False)
```

```python
import functools
import math

import jax
import jax.numpy as jnp
from jax import lax
from jax.experimental import pallas as pl
from jax.experimental.pallas import tpu as pltpu
from jax.sharding import PartitionSpec as P

VMEM = pl.BlockSpec(memory_space=pltpu.VMEM)
HBM = pl.BlockSpec(memory_space=pltpu.HBM)
TILE_PARAMS = pltpu.CompilerParams(vmem_limit_bytes=32 * 2**20)
SOLVE_PARAMS = pltpu.CompilerParams(vmem_limit_bytes=32 * 2**20)
LONG = pl.CostEstimate(flops=50_000_000_000, bytes_accessed=0, transcendentals=0)
SHORT = pl.CostEstimate(flops=1_000_000, bytes_accessed=0, transcendentals=0)
PANEL_UNIT = 2.0**17
NT = (((1,), (1,)), ((), ()))
TN = (((0,), (0,)), ((), ()))
NN = (((1,), (0,)), ((), ()))


def dot(a, b, dims):
    return lax.dot_general(a, b, dims, preferred_element_type=jnp.float32)


def halves(a):
    high = a.astype(jnp.bfloat16)
    return high, (a - high.astype(jnp.float32)).astype(jnp.bfloat16)


def dot32(a, b, dims):
    (a_high, a_low), (b_high, b_low) = halves(a), halves(b)
    return dot(a_high, b_high, dims) + (dot(a_low, b_high, dims) + dot(a_high, b_low, dims))


def chip_offset(step, core):
    swapped = {1: 2, 2: 1}.get(step, step)
    return step + core * (swapped - step)


def start_all(pairs, sems):
    copies = [pltpu.make_async_copy(source, target, sems.at[i]) for i, (source, target) in enumerate(pairs)]
    for copy in copies:
        copy.start()
    return copies


def wait_all(copies):
    for copy in copies:
        copy.wait()


def cut_kernel(n_row, targets_hbm, mine_ref, half_ref, sems):
    row = lax.axis_index("row")
    (_, width), (_, half) = mine_ref.shape, half_ref.shape
    mine = pl.ds(pl.multiple_of((row // 2) * width, width), width)
    core = pl.ds(pl.multiple_of((row % 2) * half, half), half)
    wait_all(start_all([(targets_hbm.at[:, mine], mine_ref), (targets_hbm.at[:, core], half_ref)], sems))


def mark_kernel(value_ref, out_ref):
    out_ref[...] = value_ref[0, :8, :128]


def mine_tile_kernel(scale, n_row, own_hbm, support_ref, _, *refs):
    planes = (len(refs) - 3) // (n_row // 2 + 1)
    far, outs, (targets_ref, sems) = refs[:-3 - planes], refs[-3 - planes:-2], refs[-2:]
    rows = own_hbm.shape[0]
    loads = [(own_hbm, targets_ref.at[pl.ds(0, rows)])] + far_loads(n_row, rows, far, targets_ref, 1)
    wait_all(start_all(loads, sems))
    kernel = jnp.exp(scale * dot(targets_ref[...], support_ref[...], NT))
    for plane, out_ref in enumerate(outs):
        out_ref[...] = kernel[plane * rows:(plane + 1) * rows]


def far_loads(n_row, rows, far, targets_ref, first):
    chip, width = lax.axis_index("row") // 2, far[0].shape[1]
    loads = []
    for i, piece in enumerate(far):
        plane, step = divmod(i, n_row // 2)
        cols = pl.ds(pl.multiple_of((chip ^ step) * width, width), width)
        loads.append((piece, targets_ref.at[pl.ds((first + plane) * rows, rows), cols]))
    return loads


def other_tile_kernel(scale, n_row, support_ref, *refs):
    planes = (len(refs) - 6) // (n_row // 2 + 1)
    near, far, refs = refs[:2], refs[2:-4 - planes], refs[-4 - planes:]
    outs, (targets_ref, sems) = refs[:-2], refs[-2:]
    rows, half = near[0].shape
    row = lax.axis_index("row")
    loads = far_loads(n_row, rows, far, targets_ref, 1)
    for part in range(2):
        cols = pl.ds(pl.multiple_of((row % 2 ^ part) * half, half), half)
        loads.append((near[part], targets_ref.at[pl.ds(0, rows), cols]))
    wait_all(start_all(loads, sems))
    kernel = jnp.exp(scale * dot(targets_ref[...], support_ref[...], NT))
    starts = [0, rows // 2, *range(rows, targets_ref.shape[0], rows)]
    for start, out_ref in zip(starts, outs):
        out_ref[...] = kernel[start:start + out_ref.shape[0]]


def plane_offsets(n_col, core):
    return [0, 1] + [2 * pair + 2 + core for pair in range(n_col // 2 - 1)] + [
        2 * pair + 3 - core for pair in range(n_col // 2 - 1)
    ]


def mix_kernel(corner_ref, inverse_ref, out_ref):
    out_ref[...] = dot32(dot32(inverse_ref[0], corner_ref[...], TN), inverse_ref[1], NT)


def base_kernel(mine_ref, inverse_ref, out_ref):
    out_ref[...] = dot32(mine_ref[...], inverse_ref[lax.axis_index("row") % 2], NT)


def head_kernel(base_ref, other_ref, mix_ref, out_ref):
    other = jnp.where(lax.axis_index("row") % 2 == 1, other_ref[...], 0.0)
    out_ref[...] = base_ref[...] - dot32(other, mix_ref[...], NN)


def mine_kernel(n_col, *refs):
    tiles, refs = [ref[...] for ref in refs[:n_col + 1]], refs[n_col + 1:]
    tiles[1:3] = [jnp.concatenate(tiles[1:3], axis=0)]
    own_ref, panels_ref, mine_ref, out_ref = refs
    span = own_ref.shape[2]
    row, col = lax.axis_index("row"), lax.axis_index("col")
    for step, offset in enumerate(plane_offsets(n_col, row % 2)):
        plane = col ^ offset
        block = own_ref if step == 0 else panels_ref.at[plane]
        value = tiles[step] - dot32(mine_ref[...], block[row % 2], NN)
        out_ref[:, pl.ds(pl.multiple_of(plane * span, span), span)] = value


def other_kernel(n_col, pivot, part_ref, own_ref, panels_ref, mine_ref, other_ref, out_ref):
    span = own_ref.shape[2]
    row, col = lax.axis_index("row"), lax.axis_index("col")
    for step in range(n_col):
        plane = col ^ step
        block = own_ref if step == 0 else panels_ref.at[plane]
        cols = pl.ds(pl.multiple_of(plane * span, span), span)
        out_ref[:, cols] = part_ref[:, cols] - dot32(other_ref[...], block[1 - row % 2], NN)

    @pl.when(row < 2)
    def _():
        out_ref[:, :pivot] = mine_ref[...]


def exchange(value, axis, size, mask):
    return lax.ppermute(value, axis, [(i, i ^ mask) for i in range(size)])


def exchange_chips(value, n_row, n_col, step):
    return lax.ppermute(value, ("row", "col"), [
        (r * n_col + c, (r ^ (2 * chip_offset(step, r % 2))) * n_col + c) for r in range(n_row) for c in range(n_col)
    ])


def together(*values):
    return lax.optimization_barrier(values)


def shards(support, targets, panels, diag_inverses, *, n_row, n_col):
    rows, features = targets.shape
    span = support.shape[0]
    pivot = diag_inverses.shape[1]
    scale = 0.5 / math.sqrt(features)
    row, col = lax.axis_index("row"), lax.axis_index("col")
    width = 2 * features // n_row

    mine, half = pl.pallas_call(
        functools.partial(cut_kernel, n_row),
        out_shape=[
            jax.ShapeDtypeStruct((rows, width), targets.dtype),
            jax.ShapeDtypeStruct((rows, features // 2), targets.dtype),
        ],
        in_specs=[HBM],
        out_specs=[VMEM] * 2,
        scratch_shapes=[pltpu.SemaphoreType.DMA((2,))],
        compiler_params=SOLVE_PARAMS,
        cost_estimate=SHORT,
        name="cut_kernel",
    )(targets)
    near = exchange(half, "col", n_col, 1)
    far = [
        lax.ppermute(mine, ("row", "col"), [
            (r * n_col + c, r * n_col + (c ^ (j + r % 2))) for r in range(n_row) for c in range(n_col)
        ])
        for j in range(2, n_col, 2)
    ]
    small = jnp.concatenate([panels * PANEL_UNIT] * n_col, axis=0).astype(jnp.float16)
    small = small.reshape(n_col, *panels.shape)
    blocks = lax.all_to_all(small, "col", 0, 0)
    mark = pl.pallas_call(
        mark_kernel,
        grid=(1,),
        out_shape=jax.ShapeDtypeStruct((8, 128), jnp.float32),
        in_specs=[pl.BlockSpec((1, 8, 128), lambda i: (0, 0, 0))],
        out_specs=VMEM,
        compiler_params=SOLVE_PARAMS,
        cost_estimate=LONG,
        name="mark_kernel",
    )(diag_inverses)
    far, mark = together(far, mark)
    near = [near, exchange(near, "row", n_row, 1)]
    mine_far = [
        piece for own in far for piece in [own] + [exchange(own, "row", n_row, i) for i in range(2, n_row, 2)]
    ]
    other_far = [exchange(piece, "row", n_row, 1) for piece in mine_far]

    def tile_call(body, name, counts, *operands):
        pieces = len(operands) - 1
        return list(pl.pallas_call(
            functools.partial(body, scale, n_row),
            out_shape=[jax.ShapeDtypeStruct((count, span), jnp.float32) for count in counts],
            in_specs=[VMEM if operand is support else HBM for operand in operands],
            out_specs=[VMEM] * len(counts),
            scratch_shapes=[
                pltpu.VMEM(((1 + len(far)) * rows, features), jnp.bfloat16),
                pltpu.SemaphoreType.DMA((pieces,)),
            ],
            compiler_params=TILE_PARAMS,
            cost_estimate=SHORT,
            name=name,
        )(*operands))

    first = tile_call(
        mine_tile_kernel, "mine_tile_kernel", [rows] * (1 + len(far)), targets, support, mark, *mine_far
    )
    first[0], *other_far = together(first[0], *other_far)
    last = tile_call(
        other_tile_kernel, "other_tile_kernel", [rows // 2] * 2 + [rows] * len(far), support, *near, *other_far
    )
    made = [first[0], *last[:2], *first[1:], *last[2:]]

    tiles = [made[0]] + [exchange(tile, "col", n_col, 1) for tile in made[1:3]]
    for i, tile in enumerate(made[3:]):
        turn, pair = divmod(i, len(far))
        tiles.append(lax.ppermute(tile, ("row", "col"), [
            (r * n_col + c, r * n_col + (c ^ (2 * pair + 2 + (r + turn) % 2))) for r in range(n_row) for c in range(n_col)
        ]))
    tiles, blocks = together(tiles, blocks)
    corner = blocks[0, 0, :, :pivot].astype(jnp.float32) * (1 / PANEL_UNIT)
    heads = [tile[:, :pivot] for tile in tiles]
    heads[1:3] = [jnp.concatenate(heads[1:3], axis=0)]
    head = heads[0]
    for offset, value in zip(plane_offsets(n_col, row % 2)[1:], heads[1:]):
        head = jnp.where(col == offset, value, head)
    mix = pl.pallas_call(
        mix_kernel,
        out_shape=jax.ShapeDtypeStruct((pivot, pivot), jnp.float32),
        in_specs=[VMEM] * 2,
        out_specs=VMEM,
        compiler_params=SOLVE_PARAMS,
        cost_estimate=SHORT,
        name="mix_kernel",
    )(corner, diag_inverses)
    base = pl.pallas_call(
        base_kernel,
        out_shape=jax.ShapeDtypeStruct((rows, pivot), jnp.float32),
        in_specs=[VMEM] * 2,
        out_specs=VMEM,
        compiler_params=SOLVE_PARAMS,
        cost_estimate=SHORT,
        name="base_kernel",
    )(head, diag_inverses)
    head = pl.pallas_call(
        head_kernel,
        out_shape=jax.ShapeDtypeStruct((rows, pivot), jnp.float32),
        in_specs=[VMEM] * 3,
        out_specs=VMEM,
        compiler_params=SOLVE_PARAMS,
        cost_estimate=SHORT,
        name="head_kernel",
    )(base, exchange(head, "row", n_row, 1), mix)
    spread = head
    for step in range(1, n_row // 2):
        moved = exchange_chips(head, n_row, n_col, step)
        spread = jnp.where(row // 2 == chip_offset(step, row % 2), moved, spread)
    swapped = exchange(spread, "row", n_row, 1)
    blocks = blocks.astype(jnp.float32) * (1 / PANEL_UNIT)

    part = pl.pallas_call(
        functools.partial(mine_kernel, n_col),
        out_shape=jax.ShapeDtypeStruct((rows, span * n_col), jnp.float32),
        in_specs=[VMEM] * (n_col + 4),
        out_specs=VMEM,
        compiler_params=SOLVE_PARAMS,
        cost_estimate=SHORT,
        name="mine_kernel",
    )(*tiles, panels, blocks, spread)
    return pl.pallas_call(
        functools.partial(other_kernel, n_col, pivot),
        out_shape=jax.ShapeDtypeStruct((rows, span * n_col), jnp.float32),
        in_specs=[VMEM] * 5,
        out_specs=VMEM,
        compiler_params=SOLVE_PARAMS,
        cost_estimate=SHORT,
        name="other_kernel",
    )(part, panels, blocks, spread, swapped)


def solution(mesh):
    in_specs = (P(("row", "col"), None), P("col", None), P(None, None, ("row", "col")), P())
    body = functools.partial(shards, n_row=mesh.shape["row"], n_col=mesh.shape["col"])
    return jax.shard_map(body, mesh=mesh, in_specs=in_specs, out_specs=P("col", "row"), check_vma=False)
```

```python
import functools
import math

import jax
import jax.numpy as jnp
from jax import lax
from jax.experimental import pallas as pl
from jax.experimental.pallas import tpu as pltpu
from jax.sharding import PartitionSpec as P

VMEM = pl.BlockSpec(memory_space=pltpu.VMEM)
HBM = pl.BlockSpec(memory_space=pltpu.HBM)
TILE_PARAMS = pltpu.CompilerParams(vmem_limit_bytes=32 * 2**20)
SOLVE_PARAMS = pltpu.CompilerParams(vmem_limit_bytes=32 * 2**20)
LONG = pl.CostEstimate(flops=50_000_000_000, bytes_accessed=0, transcendentals=0)
SHORT = pl.CostEstimate(flops=1_000_000, bytes_accessed=0, transcendentals=0)
PANEL_UNIT = 2.0**17
NT = (((1,), (1,)), ((), ()))
TN = (((0,), (0,)), ((), ()))
NN = (((1,), (0,)), ((), ()))


def dot(a, b, dims):
    return lax.dot_general(a, b, dims, preferred_element_type=jnp.float32)


def halves(a):
    high = a.astype(jnp.bfloat16)
    return high, (a - high.astype(jnp.float32)).astype(jnp.bfloat16)


def dot32(a, b, dims):
    (a_high, a_low), (b_high, b_low) = halves(a), halves(b)
    return dot(a_high, b_high, dims) + (dot(a_low, b_high, dims) + dot(a_high, b_low, dims))


def chip_offset(step, core):
    swapped = {1: 2, 2: 1}.get(step, step)
    return step + core * (swapped - step)


def start_all(pairs, sems):
    copies = [pltpu.make_async_copy(source, target, sems.at[i]) for i, (source, target) in enumerate(pairs)]
    for copy in copies:
        copy.start()
    return copies


def wait_all(copies):
    for copy in copies:
        copy.wait()


def cut_kernel(n_row, targets_hbm, mine_ref, half_ref, sems):
    row = lax.axis_index("row")
    (_, width), (_, half) = mine_ref.shape, half_ref.shape
    mine = pl.ds(pl.multiple_of((row // 2) * width, width), width)
    core = pl.ds(pl.multiple_of((row % 2) * half, half), half)
    wait_all(start_all([(targets_hbm.at[:, mine], mine_ref), (targets_hbm.at[:, core], half_ref)], sems))


def mark_kernel(value_ref, out_ref):
    out_ref[...] = value_ref[0, :8, :128]


def mine_tile_kernel(scale, n_row, support_ref, _, *refs):
    planes = (len(refs) - 2) // (n_row // 2 + 1)
    far, outs, (targets_ref, sems) = refs[:-2 - planes], refs[-2 - planes:-2], refs[-2:]
    rows = outs[0].shape[0]
    wait_all(start_all(far_loads(n_row, rows, far, targets_ref, 0), sems))
    kernel = jnp.exp(scale * dot(targets_ref[pl.ds(0, planes * rows)], support_ref[...], NT))
    for plane, out_ref in enumerate(outs):
        out_ref[...] = kernel[plane * rows:(plane + 1) * rows]


def far_loads(n_row, rows, far, targets_ref, first):
    chip, width = lax.axis_index("row") // 2, far[0].shape[1]
    loads = []
    for i, piece in enumerate(far):
        plane, step = divmod(i, n_row // 2)
        cols = pl.ds(pl.multiple_of((chip ^ step) * width, width), width)
        loads.append((piece, targets_ref.at[pl.ds((first + plane) * rows, rows), cols]))
    return loads


def other_tile_kernel(scale, n_row, own_hbm, support_ref, *refs):
    planes = (len(refs) - 7) // (n_row // 2 + 1)
    near, far, refs = refs[:2], refs[2:-5 - planes], refs[-5 - planes:]
    outs, (targets_ref, sems) = refs[:-2], refs[-2:]
    rows, half = near[0].shape
    row = lax.axis_index("row")
    loads = far_loads(n_row, rows, far, targets_ref, 1)
    loads.append((own_hbm, targets_ref.at[pl.ds((1 + planes) * rows, rows)]))
    for part in range(2):
        cols = pl.ds(pl.multiple_of((row % 2 ^ part) * half, half), half)
        loads.append((near[part], targets_ref.at[pl.ds(0, rows), cols]))
    wait_all(start_all(loads, sems))
    kernel = jnp.exp(scale * dot(targets_ref[...], support_ref[...], NT))
    starts = [0, rows // 2, *range(rows, targets_ref.shape[0], rows)]
    for start, out_ref in zip(starts, outs):
        out_ref[...] = kernel[start:start + out_ref.shape[0]]


def plane_offsets(n_col, core):
    return [0, 1] + [2 * pair + 2 + core for pair in range(n_col // 2 - 1)] + [
        2 * pair + 3 - core for pair in range(n_col // 2 - 1)
    ]


def mix_kernel(corner_ref, inverse_ref, out_ref):
    out_ref[...] = dot32(dot32(inverse_ref[0], corner_ref[...], TN), inverse_ref[1], NT)


def base_kernel(mine_ref, inverse_ref, out_ref):
    out_ref[...] = dot32(mine_ref[...], inverse_ref[lax.axis_index("row") % 2], NT)


def head_kernel(base_ref, other_ref, mix_ref, out_ref):
    other = jnp.where(lax.axis_index("row") % 2 == 1, other_ref[...], 0.0)
    out_ref[...] = base_ref[...] - dot32(other, mix_ref[...], NN)


def mine_kernel(n_col, *refs):
    tiles, refs = [ref[...] for ref in refs[:n_col + 1]], refs[n_col + 1:]
    tiles[1:3] = [jnp.concatenate(tiles[1:3], axis=0)]
    own_ref, panels_ref, mine_ref, out_ref = refs
    span = own_ref.shape[2]
    row, col = lax.axis_index("row"), lax.axis_index("col")
    for step, offset in enumerate(plane_offsets(n_col, row % 2)):
        plane = col ^ offset
        block = own_ref if step == 0 else panels_ref.at[plane]
        value = tiles[step] - dot32(mine_ref[...], block[row % 2], NN)
        out_ref[:, pl.ds(pl.multiple_of(plane * span, span), span)] = value


def other_kernel(n_col, pivot, part_ref, own_ref, panels_ref, mine_ref, other_ref, out_ref):
    span = own_ref.shape[2]
    row, col = lax.axis_index("row"), lax.axis_index("col")
    for step in range(n_col):
        plane = col ^ step
        block = own_ref if step == 0 else panels_ref.at[plane]
        cols = pl.ds(pl.multiple_of(plane * span, span), span)
        out_ref[:, cols] = part_ref[:, cols] - dot32(other_ref[...], block[1 - row % 2], NN)

    @pl.when(row < 2)
    def _():
        out_ref[:, :pivot] = mine_ref[...]


def exchange(value, axis, size, mask):
    return lax.ppermute(value, axis, [(i, i ^ mask) for i in range(size)])


def exchange_chips(value, n_row, n_col, step):
    return lax.ppermute(value, ("row", "col"), [
        (r * n_col + c, (r ^ (2 * chip_offset(step, r % 2))) * n_col + c) for r in range(n_row) for c in range(n_col)
    ])


def together(*values):
    return lax.optimization_barrier(values)


def shards(support, targets, panels, diag_inverses, *, n_row, n_col):
    rows, features = targets.shape
    span = support.shape[0]
    pivot = diag_inverses.shape[1]
    scale = 0.5 / math.sqrt(features)
    row, col = lax.axis_index("row"), lax.axis_index("col")
    width = 2 * features // n_row

    small = (panels * PANEL_UNIT).astype(jnp.float16)
    targets, small = together(targets, small)
    mine, half = pl.pallas_call(
        functools.partial(cut_kernel, n_row),
        out_shape=[
            jax.ShapeDtypeStruct((rows, width), targets.dtype),
            jax.ShapeDtypeStruct((rows, features // 2), targets.dtype),
        ],
        in_specs=[HBM],
        out_specs=[VMEM] * 2,
        scratch_shapes=[pltpu.SemaphoreType.DMA((2,))],
        compiler_params=SOLVE_PARAMS,
        cost_estimate=SHORT,
        name="cut_kernel",
    )(targets)
    near = exchange(half, "col", n_col, 1)
    far = [
        lax.ppermute(mine, ("row", "col"), [
            (r * n_col + c, r * n_col + (c ^ (j + r % 2))) for r in range(n_row) for c in range(n_col)
        ])
        for j in range(2, n_col, 2)
    ]
    small = jnp.concatenate([small] * n_col, axis=0).reshape(n_col, *panels.shape)
    blocks = lax.all_to_all(small, "col", 0, 0)
    mark = pl.pallas_call(
        mark_kernel,
        grid=(1,),
        out_shape=jax.ShapeDtypeStruct((8, 128), jnp.float32),
        in_specs=[pl.BlockSpec((1, 8, 128), lambda i: (0, 0, 0))],
        out_specs=VMEM,
        compiler_params=SOLVE_PARAMS,
        cost_estimate=LONG,
        name="mark_kernel",
    )(diag_inverses)
    far, mark = together(far, mark)
    near = [near, exchange(near, "row", n_row, 1)]
    mine_far = [
        piece for own in far for piece in [own] + [exchange(own, "row", n_row, i) for i in range(2, n_row, 2)]
    ]
    other_far = [exchange(piece, "row", n_row, 1) for piece in mine_far]

    def tile_call(body, name, counts, *operands):
        pieces = len(operands) - 1
        return list(pl.pallas_call(
            functools.partial(body, scale, n_row),
            out_shape=[jax.ShapeDtypeStruct((count, span), jnp.float32) for count in counts],
            in_specs=[VMEM if operand is support else HBM for operand in operands],
            out_specs=[VMEM] * len(counts),
            scratch_shapes=[
                pltpu.VMEM(((2 + len(far)) * rows, features), jnp.bfloat16),
                pltpu.SemaphoreType.DMA((pieces,)),
            ],
            compiler_params=TILE_PARAMS,
            cost_estimate=SHORT,
            name=name,
        )(*operands))

    first = tile_call(
        mine_tile_kernel, "mine_tile_kernel", [rows] * len(far), support, mark, *mine_far
    )
    first[0], *other_far = together(first[0], *other_far)
    last = tile_call(
        other_tile_kernel, "other_tile_kernel", [rows // 2] * 2 + [rows] * (1 + len(far)), targets, support, *near, *other_far
    )
    made = [last[-1], *last[:2], *first, *last[2:-1]]

    tiles = [made[0]] + [exchange(tile, "col", n_col, 1) for tile in made[1:3]]
    for i, tile in enumerate(made[3:]):
        turn, pair = divmod(i, len(far))
        tiles.append(lax.ppermute(tile, ("row", "col"), [
            (r * n_col + c, r * n_col + (c ^ (2 * pair + 2 + (r + turn) % 2))) for r in range(n_row) for c in range(n_col)
        ]))
    tiles, blocks = together(tiles, blocks)
    corner = blocks[0, 0, :, :pivot].astype(jnp.float32) * (1 / PANEL_UNIT)
    heads = [tile[:, :pivot] for tile in tiles]
    heads[1:3] = [jnp.concatenate(heads[1:3], axis=0)]
    head = heads[0]
    for offset, value in zip(plane_offsets(n_col, row % 2)[1:], heads[1:]):
        head = jnp.where(col == offset, value, head)
    mix = pl.pallas_call(
        mix_kernel,
        out_shape=jax.ShapeDtypeStruct((pivot, pivot), jnp.float32),
        in_specs=[VMEM] * 2,
        out_specs=VMEM,
        compiler_params=SOLVE_PARAMS,
        cost_estimate=SHORT,
        name="mix_kernel",
    )(corner, diag_inverses)
    base = pl.pallas_call(
        base_kernel,
        out_shape=jax.ShapeDtypeStruct((rows, pivot), jnp.float32),
        in_specs=[VMEM] * 2,
        out_specs=VMEM,
        compiler_params=SOLVE_PARAMS,
        cost_estimate=SHORT,
        name="base_kernel",
    )(head, diag_inverses)
    head = pl.pallas_call(
        head_kernel,
        out_shape=jax.ShapeDtypeStruct((rows, pivot), jnp.float32),
        in_specs=[VMEM] * 3,
        out_specs=VMEM,
        compiler_params=SOLVE_PARAMS,
        cost_estimate=SHORT,
        name="head_kernel",
    )(base, exchange(head, "row", n_row, 1), mix)
    spread = head
    for step in range(1, n_row // 2):
        moved = exchange_chips(head, n_row, n_col, step)
        spread = jnp.where(row // 2 == chip_offset(step, row % 2), moved, spread)
    swapped = exchange(spread, "row", n_row, 1)
    blocks = blocks.astype(jnp.float32) * (1 / PANEL_UNIT)

    part = pl.pallas_call(
        functools.partial(mine_kernel, n_col),
        out_shape=jax.ShapeDtypeStruct((rows, span * n_col), jnp.float32),
        in_specs=[VMEM] * (n_col + 4),
        out_specs=VMEM,
        compiler_params=SOLVE_PARAMS,
        cost_estimate=SHORT,
        name="mine_kernel",
    )(*tiles, panels, blocks, spread)
    return pl.pallas_call(
        functools.partial(other_kernel, n_col, pivot),
        out_shape=jax.ShapeDtypeStruct((rows, span * n_col), jnp.float32),
        in_specs=[VMEM] * 5,
        out_specs=VMEM,
        compiler_params=SOLVE_PARAMS,
        cost_estimate=SHORT,
        name="other_kernel",
    )(part, panels, blocks, spread, swapped)


def solution(mesh):
    in_specs = (P(("row", "col"), None), P("col", None), P(None, None, ("row", "col")), P())
    body = functools.partial(shards, n_row=mesh.shape["row"], n_col=mesh.shape["col"])
    return jax.shard_map(body, mesh=mesh, in_specs=in_specs, out_specs=P("col", "row"), check_vma=False)
```

```python
import functools
import math

import jax
import jax.numpy as jnp
from jax import lax
from jax.experimental import pallas as pl
from jax.experimental.pallas import tpu as pltpu
from jax.sharding import PartitionSpec as P

VMEM = pl.BlockSpec(memory_space=pltpu.VMEM)
HBM = pl.BlockSpec(memory_space=pltpu.HBM)
TILE_PARAMS = pltpu.CompilerParams(vmem_limit_bytes=32 * 2**20)
SOLVE_PARAMS = pltpu.CompilerParams(vmem_limit_bytes=32 * 2**20)
LONG = pl.CostEstimate(flops=50_000_000_000, bytes_accessed=0, transcendentals=0)
SHORT = pl.CostEstimate(flops=1_000_000, bytes_accessed=0, transcendentals=0)
PANEL_UNIT = 2.0**17
NT = (((1,), (1,)), ((), ()))
TN = (((0,), (0,)), ((), ()))
NN = (((1,), (0,)), ((), ()))


def dot(a, b, dims):
    return lax.dot_general(a, b, dims, preferred_element_type=jnp.float32)


def halves(a):
    high = a.astype(jnp.bfloat16)
    return high, (a - high.astype(jnp.float32)).astype(jnp.bfloat16)


def dot32(a, b, dims):
    (a_high, a_low), (b_high, b_low) = halves(a), halves(b)
    return dot(a_high, b_high, dims) + (dot(a_low, b_high, dims) + dot(a_high, b_low, dims))


def start_all(pairs, sems):
    copies = [pltpu.make_async_copy(source, target, sems.at[i]) for i, (source, target) in enumerate(pairs)]
    for copy in copies:
        copy.start()
    return copies


def wait_all(copies):
    for copy in copies:
        copy.wait()


def cut_kernel(n_row, targets_hbm, mine_ref, half_ref, sems):
    row = lax.axis_index("row")
    (_, width), (_, half) = mine_ref.shape, half_ref.shape
    mine = pl.ds(pl.multiple_of((row // 2) * width, width), width)
    core = pl.ds(pl.multiple_of((row % 2) * half, half), half)
    wait_all(start_all([(targets_hbm.at[:, mine], mine_ref), (targets_hbm.at[:, core], half_ref)], sems))


def mark_kernel(value_ref, out_ref):
    out_ref[...] = value_ref[0, :8, :128]


def mine_tile_kernel(scale, n_row, own_hbm, support_ref, _, *refs):
    planes = (len(refs) - 3) // (n_row // 2 + 1)
    far, outs, (targets_ref, sems) = refs[:-3 - planes], refs[-3 - planes:-2], refs[-2:]
    rows = own_hbm.shape[0]
    loads = [(own_hbm, targets_ref.at[pl.ds(0, rows)])] + far_loads(n_row, rows, far, targets_ref, 1)
    wait_all(start_all(loads, sems))
    kernel = jnp.exp(scale * dot(targets_ref[...], support_ref[...], NT))
    for plane, out_ref in enumerate(outs):
        out_ref[...] = kernel[plane * rows:(plane + 1) * rows]


def far_loads(n_row, rows, far, targets_ref, first):
    chip, width = lax.axis_index("row") // 2, far[0].shape[1]
    loads = []
    for i, piece in enumerate(far):
        plane, step = divmod(i, n_row // 2)
        cols = pl.ds(pl.multiple_of((chip ^ step) * width, width), width)
        loads.append((piece, targets_ref.at[pl.ds((first + plane) * rows, rows), cols]))
    return loads


def other_tile_kernel(scale, n_row, support_ref, *refs):
    planes = (len(refs) - 6) // (n_row // 2 + 1)
    near, far, refs = refs[:2], refs[2:-4 - planes], refs[-4 - planes:]
    outs, (targets_ref, sems) = refs[:-2], refs[-2:]
    rows, half = near[0].shape
    row = lax.axis_index("row")
    loads = far_loads(n_row, rows, far, targets_ref, 1)
    for part in range(2):
        cols = pl.ds(pl.multiple_of((row % 2 ^ part) * half, half), half)
        loads.append((near[part], targets_ref.at[pl.ds(0, rows), cols]))
    wait_all(start_all(loads, sems))
    kernel = jnp.exp(scale * dot(targets_ref[...], support_ref[...], NT))
    pivot = outs[0].shape[1]
    outs[0][...], outs[1][...] = kernel[:rows, :pivot], kernel[:rows, pivot:]
    for plane, out_ref in enumerate(outs[2:]):
        out_ref[...] = kernel[(1 + plane) * rows:(2 + plane) * rows]


def plane_offsets(n_col, core):
    return [0, 1] + [2 * pair + 2 + core for pair in range(n_col // 2 - 1)] + [
        2 * pair + 3 - core for pair in range(n_col // 2 - 1)
    ]


def mix_kernel(corner_ref, inverse_ref, out_ref):
    out_ref[...] = dot32(dot32(inverse_ref[0], corner_ref[...], TN), inverse_ref[1], NT)


def base_kernel(mine_ref, inverse_ref, out_ref):
    out_ref[...] = dot32(mine_ref[...], inverse_ref[lax.axis_index("row") % 2], NT)


def head_kernel(base_ref, other_ref, mix_ref, out_ref):
    other = jnp.where(lax.axis_index("row") % 2 == 1, other_ref[...], 0.0)
    out_ref[...] = base_ref[...] - dot32(other, mix_ref[...], NN)


def mine_kernel(n_col, *refs):
    tiles, refs = [ref[...] for ref in refs[:n_col + 1]], refs[n_col + 1:]
    tiles[1:3] = [jnp.concatenate(tiles[1:3], axis=1)]
    own_ref, panels_ref, mine_ref, out_ref = refs
    span = own_ref.shape[2]
    row, col = lax.axis_index("row"), lax.axis_index("col")
    for step, offset in enumerate(plane_offsets(n_col, row % 2)):
        plane = col ^ offset
        block = own_ref if step == 0 else panels_ref.at[plane]
        value = tiles[step] - dot32(mine_ref[...], block[row % 2], NN)
        out_ref[:, pl.ds(pl.multiple_of(plane * span, span), span)] = value


def other_kernel(n_col, pivot, part_ref, own_ref, panels_ref, mine_ref, other_ref, out_ref):
    span = own_ref.shape[2]
    row, col = lax.axis_index("row"), lax.axis_index("col")
    for step in range(n_col):
        plane = col ^ step
        block = own_ref if step == 0 else panels_ref.at[plane]
        cols = pl.ds(pl.multiple_of(plane * span, span), span)
        out_ref[:, cols] = part_ref[:, cols] - dot32(other_ref[...], block[1 - row % 2], NN)

    @pl.when(row < 2)
    def _():
        out_ref[:, :pivot] = mine_ref[...]


def exchange(value, axis, size, mask):
    return lax.ppermute(value, axis, [(i, i ^ mask) for i in range(size)])


def together(*values):
    return lax.optimization_barrier(values)


def shards(support, targets, panels, diag_inverses, *, n_row, n_col):
    rows, features = targets.shape
    span = support.shape[0]
    pivot = diag_inverses.shape[1]
    scale = 0.5 / math.sqrt(features)
    row, col = lax.axis_index("row"), lax.axis_index("col")
    width = 2 * features // n_row

    mine, half = pl.pallas_call(
        functools.partial(cut_kernel, n_row),
        out_shape=[
            jax.ShapeDtypeStruct((rows, width), targets.dtype),
            jax.ShapeDtypeStruct((rows, features // 2), targets.dtype),
        ],
        in_specs=[HBM],
        out_specs=[VMEM] * 2,
        scratch_shapes=[pltpu.SemaphoreType.DMA((2,))],
        compiler_params=SOLVE_PARAMS,
        cost_estimate=SHORT,
        name="cut_kernel",
    )(targets)
    near = exchange(half, "col", n_col, 1)
    far = [
        lax.ppermute(mine, ("row", "col"), [
            (r * n_col + c, r * n_col + (c ^ (j + r % 2))) for r in range(n_row) for c in range(n_col)
        ])
        for j in range(2, n_col, 2)
    ]
    small = jnp.concatenate([panels * PANEL_UNIT] * n_col, axis=0).astype(jnp.float16)
    small = small.reshape(n_col, *panels.shape)
    blocks = lax.all_to_all(small, "col", 0, 0)
    mark = pl.pallas_call(
        mark_kernel,
        grid=(1,),
        out_shape=jax.ShapeDtypeStruct((8, 128), jnp.float32),
        in_specs=[pl.BlockSpec((1, 8, 128), lambda i: (0, 0, 0))],
        out_specs=VMEM,
        compiler_params=SOLVE_PARAMS,
        cost_estimate=LONG,
        name="mark_kernel",
    )(diag_inverses)
    far, mark = together(far, mark)
    near = [near, exchange(near, "row", n_row, 1)]
    mine_far = [
        piece for own in far for piece in [own] + [exchange(own, "row", n_row, i) for i in range(2, n_row, 2)]
    ]
    other_far = [exchange(piece, "row", n_row, 1) for piece in mine_far]

    def tile_call(body, name, widths, *operands):
        pieces = len(operands) - 1
        return list(pl.pallas_call(
            functools.partial(body, scale, n_row),
            out_shape=[jax.ShapeDtypeStruct((rows, width), jnp.float32) for width in widths],
            in_specs=[VMEM if operand is support else HBM for operand in operands],
            out_specs=[VMEM] * len(widths),
            scratch_shapes=[
                pltpu.VMEM(((1 + len(far)) * rows, features), jnp.bfloat16),
                pltpu.SemaphoreType.DMA((pieces,)),
            ],
            compiler_params=TILE_PARAMS,
            cost_estimate=SHORT,
            name=name,
        )(*operands))

    first = tile_call(
        mine_tile_kernel, "mine_tile_kernel", [span] * (1 + len(far)), targets, support, mark, *mine_far
    )
    first[0], *other_far = together(first[0], *other_far)
    last = tile_call(
        other_tile_kernel, "other_tile_kernel", [pivot, span - pivot] + [span] * len(far), support, *near, *other_far
    )
    made = [first[0], *last[:2], *first[1:], *last[2:]]

    tiles = [made[0]] + [exchange(tile, "col", n_col, 1) for tile in made[1:3]]
    for i, tile in enumerate(made[3:]):
        turn, pair = divmod(i, len(far))
        tiles.append(lax.ppermute(tile, ("row", "col"), [
            (r * n_col + c, r * n_col + (c ^ (2 * pair + 2 + (r + turn) % 2))) for r in range(n_row) for c in range(n_col)
        ]))
    tiles, blocks = together(tiles, blocks)
    corner = blocks[0, 0, :, :pivot].astype(jnp.float32) * (1 / PANEL_UNIT)
    heads = [tile[:, :pivot] for tile in tiles]
    del heads[2]
    head = heads[0]
    for offset, value in zip(plane_offsets(n_col, row % 2)[1:], heads[1:]):
        head = jnp.where(col == offset, value, head)
    mix = pl.pallas_call(
        mix_kernel,
        out_shape=jax.ShapeDtypeStruct((pivot, pivot), jnp.float32),
        in_specs=[VMEM] * 2,
        out_specs=VMEM,
        compiler_params=SOLVE_PARAMS,
        cost_estimate=SHORT,
        name="mix_kernel",
    )(corner, diag_inverses)
    base = pl.pallas_call(
        base_kernel,
        out_shape=jax.ShapeDtypeStruct((rows, pivot), jnp.float32),
        in_specs=[VMEM] * 2,
        out_specs=VMEM,
        compiler_params=SOLVE_PARAMS,
        cost_estimate=SHORT,
        name="base_kernel",
    )(head, diag_inverses)
    head = pl.pallas_call(
        head_kernel,
        out_shape=jax.ShapeDtypeStruct((rows, pivot), jnp.float32),
        in_specs=[VMEM] * 3,
        out_specs=VMEM,
        compiler_params=SOLVE_PARAMS,
        cost_estimate=SHORT,
        name="head_kernel",
    )(base, exchange(head, "row", n_row, 1), mix)
    spread = head
    for i in range(2, n_row, 2):
        spread = jnp.where(row // 2 == i // 2, exchange(head, "row", n_row, i), spread)
    swapped = exchange(spread, "row", n_row, 1)
    blocks = blocks.astype(jnp.float32) * (1 / PANEL_UNIT)

    part = pl.pallas_call(
        functools.partial(mine_kernel, n_col),
        out_shape=jax.ShapeDtypeStruct((rows, span * n_col), jnp.float32),
        in_specs=[VMEM] * (n_col + 4),
        out_specs=VMEM,
        compiler_params=SOLVE_PARAMS,
        cost_estimate=SHORT,
        name="mine_kernel",
    )(*tiles, panels, blocks, spread)
    return pl.pallas_call(
        functools.partial(other_kernel, n_col, pivot),
        out_shape=jax.ShapeDtypeStruct((rows, span * n_col), jnp.float32),
        in_specs=[VMEM] * 5,
        out_specs=VMEM,
        compiler_params=SOLVE_PARAMS,
        cost_estimate=SHORT,
        name="other_kernel",
    )(part, panels, blocks, spread, swapped)


def solution(mesh):
    in_specs = (P(("row", "col"), None), P("col", None), P(None, None, ("row", "col")), P())
    body = functools.partial(shards, n_row=mesh.shape["row"], n_col=mesh.shape["col"])
    return jax.shard_map(body, mesh=mesh, in_specs=in_specs, out_specs=P("col", "row"), check_vma=False)
```
